32 devices in a mesh: bx: 8 (over z, y), by: 4 (over x, core).
Axes of the slice: x: 2, y: 2, z: 4, core: 2. Of those that a mesh axis runs over, the one named last changes fastest.
Arguments:
- source: float32 [8, 4, 6, 8192], P('bx', 'by'), may hold values from -6 to 6
- lists: int32 [8, 4, 4], P(None, 'by'), may hold values from 0 to 7, as said below
- voxel_slot: int32 [8, 4, 16384], P('bx', 'by'), may hold values from 0 to 3
- voxel_cell: int32 [8, 4, 16384], P('bx', 'by'), may hold values from 0 to 7038, as said below
- frac: float32 [8, 4, 3, 16384], P('bx', 'by'), may hold values from 0 to 1
- displace: float32 [3, 64, 16, 512], P(None, None, 'bx', 'by'), may hold values from -0.25 to 0.25
Outputs:
- warped: float32 [8, 4, 6, 16384], P('bx', 'by')
The draws below stay inside these ranges and needn't reach their ends.
Inputs may be any that keep to these rules, and one draw needn't show every extreme that they name: `lists`: each target block's 4 entries are distinct slab groups. `voxel_cell`: each is ix * 8 * 128 + iy * 128 + iz with ix < 7, iy < 7, iz < 127.
All inputs are finite; a program needn't handle non-finite values.
Results may differ from the reference program's by a relative error of at most 0.00007.
Values sent between devices are 32-bit elements; how exact they have to be, the bound alone decides.
No kernel may reach another device: no remote copies, remote signals or barrier semaphores. Data moves between devices by JAX's collectives and lax.ppermute only.
A program may use at most 64 MiB of HBM per device.

```python
import jax
import jax.numpy as jnp

TBX = 2
TBY = 128
DEPTH = 64
PX = 8
PY = 8
PZ = 128
STEPS = 2
SLABS = 8
K = 4
PB = 8192
VOXELS = 16384
NX = 16
NY = 512
N_BY = 4


def draw_lists(key, part):
    subkeys = jax.random.split(key, SLABS * N_BY)

    def choose_order(subkey):
        return jax.random.permutation(subkey, SLABS)
    orders = jax.vmap(choose_order)(subkeys)
    return orders[:, :K].reshape(SLABS, N_BY, K).astype(jnp.int32)


def draw_voxel_cell(key, part):
    full_shape = (SLABS, N_BY, VOXELS)
    subkeys = jax.random.split(key, 3)
    along_x = jax.random.randint(subkeys[0], full_shape, 0, PX - 1)
    along_y = jax.random.randint(subkeys[1], full_shape, 0, PY - 1)
    along_z = jax.random.randint(subkeys[2], full_shape, 0, PZ - 1)
    corner_index = along_x * PY * PZ + along_y * PZ + along_z
    highest = (PX - 2) * PY * PZ + (PY - 2) * PZ + PZ - 2
    return corner_index.at[:, :, 0].set(highest).astype(jnp.int32)


def set_ends(array, own_key, smallest, top_value):
    dims = array.shape
    spot = [jax.random.randint(jax.random.fold_in(own_key, axis), (), 0, dims[axis]) for axis in range(len(dims))]
    array = array.at[tuple(spot)].set(smallest)
    longest = dims.index(max(dims))
    spot[longest] = (spot[longest] + 1) % dims[longest]
    return array.at[tuple(spot)].set(top_value)


def block_scale(key, extent, pieces, low, largest):
    loudness = 1.0
    for position, shards_of in pieces:
        draws = jax.random.uniform(jax.random.fold_in(jax.random.fold_in(key, 6), position), (shards_of,), jnp.float32, low / len(pieces), largest / len(pieces))
        loudness = loudness * jnp.repeat(jnp.exp(draws), extent[position] // shards_of).reshape((-1,) + (1,) * (len(extent) - 1 - position))
    return loudness


def noise(stream_key, extent, deviation, limit, shards=(), kind=jnp.bfloat16):
    values = jax.random.normal(stream_key, extent, jnp.float32) * deviation
    if len(shards) > 0:
        values = block_scale(stream_key, extent, shards, -0.22, 0.18) * values
    return jnp.clip(values, min=-limit, max=limit).astype(kind)


def setup_inputs(seed: int = 0) -> dict:
    key_list = jax.random.split(jax.random.key(seed), 7)
    source = noise(key_list[0], (SLABS, N_BY, 6, PB), 1.0, 6.0, ((0, 8), (1, 4)), jnp.float32)
    lists = draw_lists(jax.random.fold_in(key_list[6], 71), 0)
    voxel_slot = set_ends(jax.random.randint(key_list[2], (SLABS, N_BY, VOXELS), 0, K), jax.random.fold_in(key_list[2], 1), 0, K - 1).astype(jnp.int32)
    voxel_cell = draw_voxel_cell(jax.random.fold_in(key_list[6], 71), 0)
    frac = jnp.clip(1.0 * jax.random.uniform(key_list[4], (SLABS, N_BY, 3, VOXELS), jnp.float32) ** block_scale(key_list[4], (SLABS, N_BY, 3, VOXELS), ((0, 8), (1, 4)), -0.2, 0.2), 0.0, 1.0)
    displace = jnp.clip(jax.random.uniform(key_list[5], (3, DEPTH, NX, NY), jnp.float32, -0.25, 0.25) * block_scale(key_list[5], (3, DEPTH, NX, NY), ((2, 8), (3, 4)), -0.4, 0.0), -0.25, 0.25)
    return {"source": source, "lists": lists, "voxel_slot": voxel_slot, "voxel_cell": voxel_cell, "frac": frac, "displace": displace}


def corner_weights(along_x, along_y, along_z):
    weights = []
    offsets = []
    for offset_x in range(2):
        for offset_y in range(2):
            for offset_z in range(2):
                weight_x = along_x if offset_x == 1 else 1.0 - along_x
                weight_y = along_y if offset_y == 1 else 1.0 - along_y
                weight_z = along_z if offset_z == 1 else 1.0 - along_z
                weights.append(weight_x * weight_y * weight_z)
                offsets.append(offset_x * PY * PZ + offset_y * PZ + offset_z)
    return weights, offsets


def gradients(padded):
    full = jnp.pad(padded, ((0, 0), (1, 1), (0, 0), (0, 0)))
    grad_x = 0.5 * (full[:, 1:-1, 2:, 1:-1] - full[:, 1:-1, :-2, 1:-1])
    grad_y = 0.5 * (full[:, 1:-1, 1:-1, 2:] - full[:, 1:-1, 1:-1, :-2])
    grad_z = 0.5 * (full[:, 2:, 1:-1, 1:-1] - full[:, :-2, 1:-1, 1:-1])
    return [grad_x, grad_y, grad_z]


def jacobian_matrix(gradient_list):
    return [[gradient_list[second_axis][first_axis] + (1.0 if first_axis == second_axis else 0.0)
             for second_axis in range(3)] for first_axis in range(3)]


def transpose_inverse(matrix):
    cof_00 = matrix[1][1] * matrix[2][2] - matrix[1][2] * matrix[2][1]
    cof_01 = -(matrix[1][0] * matrix[2][2] - matrix[1][2] * matrix[2][0])
    cof_02 = matrix[1][0] * matrix[2][1] - matrix[1][1] * matrix[2][0]
    cof_10 = -(matrix[0][1] * matrix[2][2] - matrix[0][2] * matrix[2][1])
    cof_11 = matrix[0][0] * matrix[2][2] - matrix[0][2] * matrix[2][0]
    cof_12 = -(matrix[0][0] * matrix[2][1] - matrix[0][1] * matrix[2][0])
    cof_20 = matrix[0][1] * matrix[1][2] - matrix[0][2] * matrix[1][1]
    cof_21 = -(matrix[0][0] * matrix[1][2] - matrix[0][2] * matrix[1][0])
    cof_22 = matrix[0][0] * matrix[1][1] - matrix[0][1] * matrix[1][0]
    determinant = matrix[0][0] * cof_00 + matrix[0][1] * cof_01 + matrix[0][2] * cof_02
    reciprocal = 1.0 / determinant
    return [[cof_00 * reciprocal, cof_01 * reciprocal, cof_02 * reciprocal],
            [cof_10 * reciprocal, cof_11 * reciprocal, cof_12 * reciprocal],
            [cof_20 * reciprocal, cof_21 * reciprocal, cof_22 * reciprocal]]


def polar_factor(jacobian):
    rotation = jacobian
    for repeat in range(STEPS):
        inverse = transpose_inverse(rotation)
        rotation = [[0.5 * (rotation[first_axis][second_axis] + inverse[first_axis][second_axis])
                     for second_axis in range(3)] for first_axis in range(3)]
    return rotation


def reorient(rotation, components):
    tensor = [[components[0], components[3], components[4]],
              [components[3], components[1], components[5]],
              [components[4], components[5], components[2]]]
    left = [[rotation[first_axis][0] * tensor[0][second_axis] + rotation[first_axis][1] * tensor[1][second_axis]
             + rotation[first_axis][2] * tensor[2][second_axis] for second_axis in range(3)] for first_axis in range(3)]

    def entry(first_axis, second_axis):
        return (left[first_axis][0] * rotation[second_axis][0] + left[first_axis][1] * rotation[second_axis][1]
                + left[first_axis][2] * rotation[second_axis][2])

    return [entry(0, 0), entry(1, 1), entry(2, 2), entry(0, 1), entry(0, 2), entry(1, 2)]


def reference(source, lists, voxel_slot, voxel_cell, frac, displace):
    slabs = source.shape[0]
    columns = source.shape[1]
    padded = jnp.pad(displace, ((0, 0), (0, 0), (1, 1), (1, 1)))

    def to_blocks(field):
        shaped = field.reshape(3, DEPTH, slabs, TBX, columns, TBY)
        return shaped.transpose(0, 2, 4, 1, 3, 5).reshape(3, slabs, columns, VOXELS)

    gradient_list = [to_blocks(field) for field in gradients(padded)]
    rotation = polar_factor(jacobian_matrix(gradient_list))
    source_slab = jnp.take_along_axis(lists, voxel_slot, axis=2).astype(jnp.int32)
    column_index = jnp.broadcast_to(jnp.arange(columns, dtype=jnp.int32)[None, :, None], source_slab.shape)
    weights, offsets = corner_weights(frac[:, :, 0], frac[:, :, 1], frac[:, :, 2])
    sample = jnp.zeros((slabs, columns, VOXELS, 6), jnp.float32)
    for corner in range(8):
        gathered = source[source_slab, column_index, :, voxel_cell + offsets[corner]]
        sample = sample + weights[corner][..., None] * gathered
    components = [sample[..., index] for index in range(6)]
    result = reorient(rotation, components)
    return jnp.stack(result, axis=2)
```

```python
import jax
import jax.numpy as jnp
from jax import lax
from jax.experimental import pallas as pl
from jax.experimental.pallas import tpu as pltpu
from jax.sharding import PartitionSpec as P

PX = 8
PY = 8
PZ = 128
STEPS = 2


def with_halo(cells, sides, width):
    for axis, dim in sides:
        count = lax.axis_size(axis)
        ends = count - 1
        head = lax.slice_in_dim(cells, 0, width, axis=dim)
        tail = lax.slice_in_dim(cells, cells.shape[dim] - width, cells.shape[dim], axis=dim)
        cells = jnp.concatenate(
            [
                lax.ppermute(tail, axis, [(i, (i + 1) % count) for i in range(ends)]),
                cells,
                lax.ppermute(head, axis, [((i + 1) % count, i) for i in range(ends)]),
            ],
            axis=dim,
        )
    return cells


def gradients(padded):
    full = jnp.pad(padded, ((0, 0), (1, 1), (0, 0), (0, 0)))
    grad_x = 0.5 * (full[:, 1:-1, 2:, 1:-1] - full[:, 1:-1, :-2, 1:-1])
    grad_y = 0.5 * (full[:, 1:-1, 1:-1, 2:] - full[:, 1:-1, 1:-1, :-2])
    grad_z = 0.5 * (full[:, 2:, 1:-1, 1:-1] - full[:, :-2, 1:-1, 1:-1])
    return [grad_x, grad_y, grad_z]


def jacobian_matrix(gradient_list):
    return [
        [
            gradient_list[second_axis][first_axis] + (1.0 if first_axis == second_axis else 0.0)
            for second_axis in range(3)
        ]
        for first_axis in range(3)
    ]


def transpose_inverse(matrix):
    cof_00 = matrix[1][1] * matrix[2][2] - matrix[1][2] * matrix[2][1]
    cof_01 = -(matrix[1][0] * matrix[2][2] - matrix[1][2] * matrix[2][0])
    cof_02 = matrix[1][0] * matrix[2][1] - matrix[1][1] * matrix[2][0]
    cof_10 = -(matrix[0][1] * matrix[2][2] - matrix[0][2] * matrix[2][1])
    cof_11 = matrix[0][0] * matrix[2][2] - matrix[0][2] * matrix[2][0]
    cof_12 = -(matrix[0][0] * matrix[2][1] - matrix[0][1] * matrix[2][0])
    cof_20 = matrix[0][1] * matrix[1][2] - matrix[0][2] * matrix[1][1]
    cof_21 = -(matrix[0][0] * matrix[1][2] - matrix[0][2] * matrix[1][0])
    cof_22 = matrix[0][0] * matrix[1][1] - matrix[0][1] * matrix[1][0]
    determinant = matrix[0][0] * cof_00 + matrix[0][1] * cof_01 + matrix[0][2] * cof_02
    reciprocal = 1.0 / determinant
    return [
        [cof_00 * reciprocal, cof_01 * reciprocal, cof_02 * reciprocal],
        [cof_10 * reciprocal, cof_11 * reciprocal, cof_12 * reciprocal],
        [cof_20 * reciprocal, cof_21 * reciprocal, cof_22 * reciprocal],
    ]


def polar_factor(jacobian):
    rotation = jacobian
    for repeat in range(STEPS):
        inverse = transpose_inverse(rotation)
        rotation = [
            [
                0.5 * (rotation[first_axis][second_axis] + inverse[first_axis][second_axis])
                for second_axis in range(3)
            ]
            for first_axis in range(3)
        ]
    return rotation


def reorient(rotation, components):
    tensor = [
        [components[0], components[3], components[4]],
        [components[3], components[1], components[5]],
        [components[4], components[5], components[2]],
    ]
    left = [
        [
            rotation[first_axis][0] * tensor[0][second_axis]
            + rotation[first_axis][1] * tensor[1][second_axis]
            + rotation[first_axis][2] * tensor[2][second_axis]
            for second_axis in range(3)
        ]
        for first_axis in range(3)
    ]

    def entry(first_axis, second_axis):
        return (
            left[first_axis][0] * rotation[second_axis][0]
            + left[first_axis][1] * rotation[second_axis][1]
            + left[first_axis][2] * rotation[second_axis][2]
        )

    return [entry(0, 0), entry(1, 1), entry(2, 2), entry(0, 1), entry(0, 2), entry(1, 2)]


def sample_kernel(slab_ref, table_ref, slot_ref, cell_ref, frac_ref, out_ref):
    slots = slab_ref.shape[0]
    groups = slot_ref.shape[0]
    row_iota = lax.broadcasted_iota(jnp.int32, (PY, PZ), 0)

    def spread(row):
        return jnp.broadcast_to(row, (PY, PZ))

    def group(g, carry):
        slot = spread(slot_ref[pl.ds(g, 1), :])
        cell = spread(cell_ref[pl.ds(g, 1), :])
        along_x = spread(frac_ref[0, pl.ds(g, 1), :])
        along_y = spread(frac_ref[1, pl.ds(g, 1), :])
        along_z = spread(frac_ref[2, pl.ds(g, 1), :])
        iz = cell & (PZ - 1)
        iy = (cell // PZ) & (PY - 1)
        ix = cell // (PY * PZ)
        weight_y = jnp.where(row_iota == iy, 1.0 - along_y, jnp.where(row_iota == iy + 1, along_y, 0.0))
        code = slot * PX + ix

        def one_slot(s, totals):
            slab = slab_ref[s]
            totals = list(totals)
            for x in range(PX):
                here = s * PX + x
                weight = jnp.where(code == here, 1.0 - along_x, 0.0)
                if x > 0:
                    weight = jnp.where(code == here - 1, along_x, weight)
                for c in range(6):
                    part = table_ref[slab, c * PX + x]
                    lower = jnp.take_along_axis(part, iz, axis=1, mode="promise_in_bounds")
                    upper = jnp.take_along_axis(part, iz + 1, axis=1, mode="promise_in_bounds")
                    totals[c] = totals[c] + weight * lower
                    totals[6 + c] = totals[6 + c] + weight * upper
            return tuple(totals)

        zero = jnp.zeros((PY, PZ), jnp.float32)
        totals = lax.fori_loop(0, slots, one_slot, (zero,) * 12)
        rows = [
            jnp.sum((totals[c] * (1.0 - along_z) + totals[6 + c] * along_z) * weight_y, axis=0, keepdims=True)
            for c in range(6)
        ]
        out_ref[pl.ds(g, 1)] = jnp.concatenate(rows, axis=0)[None]
        return carry

    lax.fori_loop(0, groups, group, 0)


def on_device(source, lists, voxel_slot, voxel_cell, frac, displace):
    count = lax.axis_size("bx")
    row_index = lax.axis_index("bx")
    voxels = voxel_cell.shape[2]
    groups = voxels // PZ
    table = source.reshape(6 * PX * PY, PZ)
    my_slabs = lax.dynamic_index_in_dim(lists[:, 0, :], row_index, 0, keepdims=False)
    line = lax.all_gather(
        table, "bx", axis=0, axis_index_groups=[list(range(k, count, 2)) for k in range(2)]
    )
    across = lax.ppermute(line, "bx", [(i, i ^ 1) for i in range(count)])
    odd = row_index % 2 == 1
    blocks = jnp.stack([jnp.where(odd, across, line), jnp.where(odd, line, across)], axis=1)
    blocks = blocks.reshape(count, 6 * PX, PY, PZ)
    vmem = pl.BlockSpec(memory_space=pltpu.VMEM)
    sample = pl.pallas_call(
        sample_kernel,
        out_shape=jax.ShapeDtypeStruct((groups, 6, PZ), jnp.float32),
        in_specs=[pl.BlockSpec(memory_space=pltpu.SMEM)] + [vmem] * 4,
        out_specs=vmem,
        compiler_params=pltpu.CompilerParams(vmem_limit_bytes=32 * 2**20),
    )(
        my_slabs,
        blocks,
        voxel_slot.reshape(groups, PZ),
        voxel_cell.reshape(groups, PZ),
        frac.reshape(3, groups, PZ),
    )
    padded = with_halo(displace, (("bx", 2), ("by", 3)), 1)
    gradient_list = [field.reshape(3, groups, PZ) for field in gradients(padded)]
    rotation = polar_factor(jacobian_matrix(gradient_list))
    result = reorient(rotation, [sample[:, index] for index in range(6)])
    return jnp.stack(result, 0).reshape(1, 1, 6, voxels)


def solution(mesh):
    return jax.shard_map(
        on_device,
        mesh=mesh,
        in_specs=(
            P("bx", "by", None, None),
            P(None, "by", None),
            P("bx", "by", None),
            P("bx", "by", None),
            P("bx", "by", None, None),
            P(None, None, "bx", "by"),
        ),
        out_specs=P("bx", "by", None, None),
        check_vma=False,
    )
```

```python
import functools

import jax
import jax.numpy as jnp
from jax import lax
from jax.experimental import pallas as pl
from jax.experimental.pallas import tpu as pltpu
from jax.sharding import PartitionSpec as P

PX = 8
PY = 8
PZ = 128
STEPS = 2
PARTS = 6
DENSE = 6
WIDE = 1024
UNROLL = 16
F32 = jnp.float32
BF16 = jnp.bfloat16
VMEM = pl.BlockSpec(memory_space=pltpu.VMEM)
SMEM = pl.BlockSpec(memory_space=pltpu.SMEM)


def kernel_call(body, outs, ins, scratch=(), aliases=None, cost=None):
    return pl.pallas_call(
        body,
        out_shape=outs,
        in_specs=ins,
        out_specs=jax.tree.map(lambda _: VMEM, outs),
        scratch_shapes=list(scratch),
        input_output_aliases=aliases or {},
        cost_estimate=cost,
        compiler_params=pltpu.CompilerParams(vmem_limit_bytes=40 * 2**20),
    )


def rank_kernel(slots, slot_ref, pos_ref, dest_ref, info_ref):
    groups = slot_ref.shape[0]
    row = lax.broadcasted_iota(jnp.int32, (PZ, PZ), 0)
    col = lax.broadcasted_iota(jnp.int32, (PZ, PZ), 1)
    before = jnp.where(row < col, 1.0, 0.0).astype(BF16)
    grow = lax.broadcasted_iota(jnp.int32, (groups, groups), 0)
    gcol = lax.broadcasted_iota(jnp.int32, (groups, groups), 1)
    gbefore = jnp.where(grow < gcol, 1.0, 0.0).astype(BF16)
    gafter = jnp.where(grow > gcol, 1.0, 0.0).astype(BF16)
    ones = jnp.ones((PZ, PZ), BF16)
    dest = jnp.zeros((groups, PZ), F32)
    pos = jnp.zeros((groups, PZ), F32)
    start = jnp.zeros((groups, PZ), F32)
    for s in range(slots):
        on = slot_ref[...] == s
        mask = jnp.where(on, 1.0, 0.0).astype(BF16)
        rank = jnp.dot(mask, before, preferred_element_type=F32)
        count = jnp.dot(mask, ones, preferred_element_type=F32)
        base = jnp.dot(gafter, count.astype(BF16), preferred_element_type=F32)
        dest = jnp.where(on, rank + start, dest)
        pos = jnp.where(on, rank + base, pos)
        start = start + count
        across = lax.dot_general(ones[:PY], mask, (((1,), (1,)), ((), ())), preferred_element_type=F32)
        ahead = jnp.dot(across.astype(BF16), gbefore, preferred_element_type=F32)
        info_ref[s : s + 1, :] = ahead[0:1].astype(jnp.int32)
        info_ref[slots + s : slots + s + 1, :] = across[0:1].astype(jnp.int32)
    pos_ref[...] = pos.astype(jnp.int32)
    dest_ref[...] = dest.astype(jnp.int32)


def sort_kernel(slots, info_ref, dest_ref, cell_ref, frac_ref, sorted_ref, load_ref, index_ref):
    groups = dest_ref.shape[0]
    for b in range(groups // 8):
        here = slice(8 * b, 8 * b + 8)
        cell = cell_ref[here, :]
        rows = [frac_ref[i, here, :] for i in range(3)]
        rows += [(cell // (PY * PZ)).astype(F32), ((cell // PZ) & (PY - 1)).astype(F32), (cell & (PZ - 1)).astype(F32)]
        for i, values in enumerate(rows):
            load_ref[pl.ds(64 * b + i, 8, stride=8), :] = values
    lane = lax.broadcasted_iota(jnp.int32, (8, PZ), 1)
    lanes = lane.astype(F32).astype(BF16)
    place = lax.broadcasted_iota(jnp.int32, (PZ, PZ), 0)

    def invert(b, carry):
        first = pl.multiple_of(b * 8, 8)
        dest = dest_ref[pl.ds(first, 8), :]
        moves = jnp.concatenate(
            [jnp.where(place == dest[j : j + 1, :], 1.0, 0.0).astype(BF16) for j in range(8)], axis=0
        )
        index = lax.dot_general(lanes, moves, (((1,), (1,)), ((), ())), preferred_element_type=F32).astype(jnp.int32)
        for j in range(8):
            index_ref[first + j] = index[:, PZ * j : PZ * j + PZ]
        return carry

    lax.fori_loop(0, groups // 8, invert, 0)

    def append(b, carry):
        rows = []
        for j in range(UNROLL):
            g = b * UNROLL + j
            values = load_ref[pl.ds(pl.multiple_of(g * 8, 8), 8), :]
            ordered = jnp.take_along_axis(values, index_ref[g], axis=1, mode="promise_in_bounds")
            start = 0
            for s in range(slots):
                base = info_ref[s, g]
                offset = base & (PZ - 1)
                rows.append((s, base // PZ, offset, pltpu.roll(ordered, (offset - start) & (PZ - 1), axis=1)))
                start = start + info_ref[slots + s, g]
        for s, at, offset, values in rows:
            pltpu.store(sorted_ref.at[s, at], values, mask=lane >= offset)
            sorted_ref[s, at + 1] = values
        return carry

    lax.fori_loop(0, groups // UNROLL, append, 0)


def fold_rows(values):
    row = lax.broadcasted_iota(jnp.int32, values[0].shape, 0)
    values = list(values) + [jnp.zeros_like(values[0])] * (8 - len(values))
    for step in (1, 2, 4):
        low = (row & step) == 0
        values = [
            jnp.where(low, a, b) + pltpu.roll(jnp.where(low, b, a), step, axis=0)
            for a, b in zip(values[0::2], values[1::2])
        ]
    return values[0]


def sample_slot(s, block_ref, total, sorted_ref, out_ref, table_ref):
    dense = PARTS * PY * DENSE
    width = PY * DENSE
    for c in range(PARTS):
        part = block_ref[c * PX * PY : c * PX * PY + width]
        high = part.astype(BF16)
        low = (part - high.astype(F32)).astype(BF16)
        at = c * width
        for k in range(2):
            table_ref[at : at + width, PZ * k : PZ * k + PZ] = high
            table_ref[dense + at : dense + at + width, PZ * k : PZ * k + PZ] = low
    per = WIDE // PZ
    row = lax.broadcasted_iota(jnp.int32, (PY, PZ), 0).astype(F32)
    depth = lax.broadcasted_iota(jnp.int32, (PZ, WIDE), 0).astype(F32).astype(BF16)

    def in_two(value):
        high = value.astype(BF16).astype(F32)
        return high, value - high

    def packed(value):
        return jnp.broadcast_to(value, (16, WIDE)).astype(BF16)[0:1]

    def step(i, carry):
        loads = [sorted_ref[s, i * per + j] for j in range(per)]
        wide = jnp.concatenate(loads, axis=1)
        along_z, iz = wide[2:3], wide[5:6]
        lower_high, lower_low = in_two(1.0 - along_z)
        upper_high, upper_low = in_two(along_z)
        none = jnp.zeros((), BF16)
        at_lower = depth == packed(iz)
        at_upper = depth == packed(iz + 1.0)
        high = jnp.where(at_lower, packed(lower_high), jnp.where(at_upper, packed(upper_high), none))
        low = jnp.where(at_lower, packed(lower_low), jnp.where(at_upper, packed(upper_low), none))
        product = jnp.dot(table_ref[...], jnp.concatenate([high, low], axis=0), preferred_element_type=F32)
        for j in range(per):
            fx, fy, fz, ix, iy, iz = [jnp.broadcast_to(loads[j][k : k + 1], (PY, PZ)) for k in range(6)]
            lower = jnp.clip(iz.astype(jnp.int32), 0, PZ - 2)
            upper = lower + 1
            weight_y = jnp.where(row == iy, 1.0 - fy, jnp.where(row == iy + 1.0, fy, 0.0))
            lanes = slice(PZ * j, PZ * j + PZ)
            totals = [None] * PARTS
            for x in range(PX):
                weight = weight_y * jnp.where(ix == float(x), 1.0 - fx, jnp.where(ix == float(x - 1), fx, 0.0))
                weight_lower, weight_upper = weight * (1.0 - fz), weight * fz
                for c in range(PARTS):
                    if x < DENSE:
                        at = c * width + x * PY
                        term = (product[at : at + PY, lanes] + product[dense + at : dense + at + PY, lanes]) * weight
                    else:
                        at = (c * PX + x) * PY
                        cells = block_ref[at : at + PY]
                        term = (
                            jnp.take_along_axis(cells, lower, axis=1, mode="promise_in_bounds") * weight_lower
                            + jnp.take_along_axis(cells, upper, axis=1, mode="promise_in_bounds") * weight_upper
                        )
                    totals[c] = term if x == 0 else totals[c] + term
            out_ref[s, i * per + j] = fold_rows(totals)
        return carry

    lax.fori_loop(0, (total + WIDE - 1) // WIDE, step, 0)


def sample_kernel(slots, first, blocks, again, plan_ref, info_ref, sorted_ref, *refs):
    block_refs = refs[:blocks]
    out_ref, table_ref = refs[blocks + again :]
    last = info_ref.shape[1] - 1
    for b in range(blocks):
        s = plan_ref[first + b]

        @pl.when(s >= 0)
        def _():
            total = info_ref[s, last] + info_ref[slots + s, last]
            sample_slot(s, block_refs[b], total, sorted_ref, out_ref, table_ref)


def sample(slots, first, blocks, plan, info, ordered, before):
    again = 0 if before is None else 1
    return kernel_call(
        functools.partial(sample_kernel, slots, first, len(blocks), again),
        jax.ShapeDtypeStruct(ordered.shape, F32),
        [SMEM, SMEM] + [VMEM] * (1 + len(blocks) + again),
        [pltpu.VMEM((2 * PARTS * PY * DENSE, 2 * PZ), BF16)],
        {3 + len(blocks): 0} if again else None,
    )(plan, info, ordered, *blocks, *([before] if again else []))


def transpose_inverse(matrix):
    cof_00 = matrix[1][1] * matrix[2][2] - matrix[1][2] * matrix[2][1]
    cof_01 = -(matrix[1][0] * matrix[2][2] - matrix[1][2] * matrix[2][0])
    cof_02 = matrix[1][0] * matrix[2][1] - matrix[1][1] * matrix[2][0]
    cof_10 = -(matrix[0][1] * matrix[2][2] - matrix[0][2] * matrix[2][1])
    cof_11 = matrix[0][0] * matrix[2][2] - matrix[0][2] * matrix[2][0]
    cof_12 = -(matrix[0][0] * matrix[2][1] - matrix[0][1] * matrix[2][0])
    cof_20 = matrix[0][1] * matrix[1][2] - matrix[0][2] * matrix[1][1]
    cof_21 = -(matrix[0][0] * matrix[1][2] - matrix[0][2] * matrix[1][0])
    cof_22 = matrix[0][0] * matrix[1][1] - matrix[0][1] * matrix[1][0]
    determinant = matrix[0][0] * cof_00 + matrix[0][1] * cof_01 + matrix[0][2] * cof_02
    reciprocal = 1.0 / determinant
    return [
        [cof_00 * reciprocal, cof_01 * reciprocal, cof_02 * reciprocal],
        [cof_10 * reciprocal, cof_11 * reciprocal, cof_12 * reciprocal],
        [cof_20 * reciprocal, cof_21 * reciprocal, cof_22 * reciprocal],
    ]


def polar_factor(jacobian):
    rotation = jacobian
    for repeat in range(STEPS):
        inverse = transpose_inverse(rotation)
        rotation = [
            [0.5 * (rotation[first][second] + inverse[first][second]) for second in range(3)] for first in range(3)
        ]
    return rotation


def reorient(rotation, components):
    tensor = [
        [components[0], components[3], components[4]],
        [components[3], components[1], components[5]],
        [components[4], components[5], components[2]],
    ]
    left = [
        [
            rotation[first][0] * tensor[0][second]
            + rotation[first][1] * tensor[1][second]
            + rotation[first][2] * tensor[2][second]
            for second in range(3)
        ]
        for first in range(3)
    ]

    def entry(first, second):
        return (
            left[first][0] * rotation[second][0]
            + left[first][1] * rotation[second][1]
            + left[first][2] * rotation[second][2]
        )

    return [entry(0, 0), entry(1, 1), entry(2, 2), entry(0, 1), entry(0, 2), entry(1, 2)]


def rotation_kernel(field_ref, left_ref, right_ref, down_ref, up_ref, out_ref, wide_ref, slope_ref, edge_ref):
    rows = field_ref.shape[1]
    edge_ref[...] = jnp.zeros_like(edge_ref)
    edge_ref[0:3, :] = down_ref[...]
    edge_ref[3:6, :] = up_ref[...]
    edges = edge_ref[...].T
    for c in range(3):
        wide_ref[c, 0:8, :] = jnp.zeros((8, PZ), F32)
        wide_ref[c, 8 : 8 + rows, :] = field_ref[c]
        wide_ref[c, 8 + rows : 16 + rows, :] = jnp.zeros((8, PZ), F32)
        even = wide_ref[c, pl.ds(8, rows // 2, stride=2), :]
        odd = wide_ref[c, pl.ds(9, rows // 2, stride=2), :]
        slope_ref[c, pl.ds(0, rows // 2, stride=2), :] = 0.5 * (odd - left_ref[c])
        slope_ref[c, pl.ds(1, rows // 2, stride=2), :] = 0.5 * (right_ref[c] - even)
    lane = lax.broadcasted_iota(jnp.int32, (16, PZ), 1)
    for b in range(rows // 16):
        jacobian = []
        for c in range(3):
            at = 16 * b
            middle = field_ref[c, at : at + 16, :]
            after = pltpu.roll(middle, PZ - 1, axis=1)
            after = jnp.where(lane == PZ - 1, edges[at : at + 16, 3 + c : 4 + c], after)
            prior = pltpu.roll(middle, 1, axis=1)
            prior = jnp.where(lane == 0, edges[at : at + 16, c : c + 1], prior)
            slopes = [
                slope_ref[c, at : at + 16, :],
                0.5 * (after - prior),
                0.5 * (wide_ref[c, at + 10 : at + 26, :] - wide_ref[c, at + 6 : at + 22, :]),
            ]
            jacobian.append([slopes[d] + 1.0 if d == c else slopes[d] for d in range(3)])
        rotation = polar_factor(jacobian)
        for first in range(3):
            for second in range(3):
                out_ref[3 * first + second, at : at + 16, :] = rotation[first][second]


def along(values, axis, pairs):
    return lax.ppermute(values, axis, pairs)


def rotations(displace):
    depth, wide = displace.shape[1], displace.shape[2]
    rows = depth * wide

    def steps(axis):
        return [(i, i + 1) for i in range(lax.axis_size(axis) - 1)]

    def back(pairs):
        return [(b, a) for a, b in pairs]

    left = along(displace[:, :, wide - 1, :], "bx", steps("bx"))
    right = along(displace[:, :, 0, :], "bx", back(steps("bx")))
    down = along(displace[:, :, :, PZ - 1].reshape(3, rows), "by", steps("by"))
    up = along(displace[:, :, :, 0].reshape(3, rows), "by", back(steps("by")))
    return kernel_call(
        rotation_kernel,
        jax.ShapeDtypeStruct((9, rows, PZ), F32),
        [VMEM] * 5,
        [
            pltpu.VMEM((3, rows + 16, PZ), F32),
            pltpu.VMEM((3, rows, PZ), F32),
            pltpu.VMEM((8, rows), F32),
        ],
    )(displace.reshape(3, rows, PZ), left, right, down, up)


def finish_kernel(slots, info_ref, slot_ref, pos_ref, samples_ref, rotation_ref, out_ref, row_ref):
    groups = slot_ref.shape[0]
    lane = lax.broadcasted_iota(jnp.int32, (8, PZ), 1)

    def step(b, carry):
        first = pl.multiple_of(b * UNROLL, UNROLL)
        slot_rows = slot_ref[pl.ds(first, UNROLL), :]
        lane_rows = pos_ref[pl.ds(first, UNROLL), :] & (PZ - 1)
        for j in range(UNROLL):
            slot = jnp.broadcast_to(slot_rows[j : j + 1], (8, PZ))
            index = jnp.broadcast_to(lane_rows[j : j + 1], (8, PZ))
            result = None
            for s in range(slots):
                base = info_ref[s, first + j]
                offset, at = base & (PZ - 1), base // PZ
                both = jnp.where(lane >= offset, samples_ref[s, at], samples_ref[s, at + 1])
                value = jnp.take_along_axis(both, index, axis=1, mode="promise_in_bounds")
                result = value if s == 0 else jnp.where(slot == s, value, result)
            row_ref[pl.ds(pl.multiple_of((first + j) * 8, 8), 8), :] = result
        for k in range(UNROLL // 8):
            at = pl.multiple_of(first + 8 * k, 8)
            components = [row_ref[pl.ds(at * 8 + c, 8, stride=8), :] for c in range(PARTS)]
            rotation = [[rotation_ref[3 * m + n, pl.ds(at, 8), :] for n in range(3)] for m in range(3)]
            for c, value in enumerate(reorient(rotation, components)):
                out_ref[c, pl.ds(at, 8), :] = value
        return carry

    lax.fori_loop(0, groups // UNROLL, step, 0)


def on_device(source, lists, voxel_slot, voxel_cell, frac, displace):
    count = lax.axis_size("bx")
    row = lax.axis_index("bx")
    lines = count // 2
    slots = lists.shape[2]
    voxels = voxel_cell.shape[2]
    groups = voxels // PZ
    table = source.reshape(PARTS * PX * PY, PZ)

    swap = [(i, i ^ 1) for i in range(count)]
    forward = [(i, (i + 2) % count) for i in range(count)]
    backward = [(b, a) for a, b in forward]
    arrivals = [(table, 0, 0), (along(table, "bx", swap), 0, 1)]
    ahead = behind = table
    for k in range(1, lines // 2 + 1):
        ahead = along(ahead, "bx", forward)
        new = [(ahead, k)]
        if k <= (lines - 1) // 2:
            behind = along(behind, "bx", backward)
            new.append((behind, -k))
        arrivals += [(b, k, 0) for b, k in new]
        arrivals += [(along(b, "bx", swap), k, 1) for b, k in new]

    my_slabs = lax.dynamic_index_in_dim(lists[:, 0, :], row, 0, keepdims=False)
    far = jnp.array([k for _, k, _ in arrivals], jnp.int32)
    over = jnp.array([k for _, _, k in arrivals], jnp.int32)
    owners = ((row // 2 - far + count) % lines) * 2 + (row % 2 + over) % 2
    listed = owners[:, None] == my_slabs[None, :]
    plan = jnp.max(jnp.where(listed, jnp.arange(slots, dtype=jnp.int32)[None, :], -1), axis=1)

    slot_rows = voxel_slot.reshape(groups, PZ)
    ints = jax.ShapeDtypeStruct((groups, PZ), jnp.int32)
    pos, dest, info = kernel_call(
        functools.partial(rank_kernel, slots),
        (ints, ints, jax.ShapeDtypeStruct((2 * slots, groups), jnp.int32)),
        [VMEM],
    )(slot_rows)
    ordered = kernel_call(
        functools.partial(sort_kernel, slots),
        jax.ShapeDtypeStruct((slots, groups + WIDE // PZ, 8, PZ), F32),
        [SMEM, VMEM, VMEM, VMEM],
        [pltpu.VMEM((groups * 8, PZ), F32), pltpu.VMEM((groups, 8, PZ), jnp.int32)],
    )(info, dest, voxel_cell.reshape(groups, PZ), frac.reshape(3, groups, PZ))
    rotation = rotations(displace)

    samples = None
    cuts = [0] + [c for c in (2, 4, count - 1, count) if c <= count]
    for first, last in zip(cuts[:-1], cuts[1:]):
        blocks = [b for b, _, _ in arrivals[first:last]]
        samples = sample(slots, first, blocks, plan, info, ordered, samples)

    result = kernel_call(
        functools.partial(finish_kernel, slots),
        jax.ShapeDtypeStruct((PARTS, groups, PZ), F32),
        [SMEM] + [VMEM] * 4,
        [pltpu.VMEM((groups * 8, PZ), F32)],
    )(info, slot_rows, pos, samples, rotation)
    return result.reshape(1, 1, PARTS, voxels)


def solution(mesh):
    return jax.shard_map(
        on_device,
        mesh=mesh,
        in_specs=(
            P("bx", "by", None, None),
            P(None, "by", None),
            P("bx", "by", None),
            P("bx", "by", None),
            P("bx", "by", None, None),
            P(None, None, "bx", "by"),
        ),
        out_specs=P("bx", "by", None, None),
        check_vma=False,
    )
```

```python
import functools

import jax
import jax.numpy as jnp
from jax import lax
from jax.experimental import pallas as pl
from jax.experimental.pallas import tpu as pltpu
from jax.sharding import PartitionSpec as P

PX = 8
PY = 8
PZ = 128
STEPS = 2
PARTS = 6
DENSE = 6
WIDE = 1024
UNROLL = 16
SHARE = 32
F32 = jnp.float32
BF16 = jnp.bfloat16
VMEM = pl.BlockSpec(memory_space=pltpu.VMEM)
SMEM = pl.BlockSpec(memory_space=pltpu.SMEM)
HBM = pl.BlockSpec(memory_space=pltpu.HBM)


def kernel_call(body, outs, ins, scratch=(), aliases=None, cost=1.0, out_spec=VMEM):
    return pl.pallas_call(
        body,
        out_shape=outs,
        in_specs=ins,
        out_specs=jax.tree.map(lambda _: out_spec, outs),
        scratch_shapes=list(scratch),
        input_output_aliases=aliases or {},
        cost_estimate=pl.CostEstimate(flops=0, bytes_accessed=int(cost * 3.0e6), transcendentals=0),
        compiler_params=pltpu.CompilerParams(vmem_limit_bytes=24 * 2**20),
    )


def ranks(slots, slot, pos_ref, dest_ref, info_ref):
    groups = slot.shape[0]
    row = lax.broadcasted_iota(jnp.int32, (PZ, PZ), 0)
    col = lax.broadcasted_iota(jnp.int32, (PZ, PZ), 1)
    before = jnp.where(row < col, 1.0, 0.0).astype(BF16)
    grow = lax.broadcasted_iota(jnp.int32, (groups, groups), 0)
    gcol = lax.broadcasted_iota(jnp.int32, (groups, groups), 1)
    gbefore = jnp.where(grow < gcol, 1.0, 0.0).astype(BF16)
    gafter = jnp.where(grow > gcol, 1.0, 0.0).astype(BF16)
    ones = jnp.ones((PZ, PZ), BF16)
    dest = jnp.zeros((groups, PZ), F32)
    pos = jnp.zeros((groups, PZ), F32)
    start = jnp.zeros((groups, PZ), F32)
    for s in range(slots):
        on = slot == s
        mask = jnp.where(on, 1.0, 0.0).astype(BF16)
        rank = jnp.dot(mask, before, preferred_element_type=F32)
        count = jnp.dot(mask, ones, preferred_element_type=F32)
        base = jnp.dot(gafter, count.astype(BF16), preferred_element_type=F32)
        dest = jnp.where(on, rank + start, dest)
        pos = jnp.where(on, rank + base, pos)
        start = start + count
        across = lax.dot_general(ones[:PY], mask, (((1,), (1,)), ((), ())), preferred_element_type=F32)
        ahead = jnp.dot(across.astype(BF16), gbefore, preferred_element_type=F32)
        info_ref[s : s + 1, :] = ahead[0:1].astype(jnp.int32)
        info_ref[slots + s : slots + s + 1, :] = across[0:1].astype(jnp.int32)
    pos_ref[...] = pos.astype(jnp.int32)
    dest_ref[...] = dest.astype(jnp.int32)


def order_kernel(
    slots, slot_hbm, cell_hbm, frac_hbm, sorted_ref, pos_ref, info_ref,
    slot_ref, cell_ref, frac_ref, dest_ref, load_ref, index_ref, table_ref, sems,
):
    groups = pos_ref.shape[0]
    loads = [
        pltpu.make_async_copy(slot_hbm, slot_ref, sems.at[0]),
        pltpu.make_async_copy(cell_hbm, cell_ref, sems.at[1]),
        pltpu.make_async_copy(frac_hbm, frac_ref, sems.at[2]),
    ]
    for load in loads:
        load.start()
    loads[0].wait()
    ranks(slots, slot_ref[...], pos_ref, dest_ref, info_ref)
    scalars = pltpu.make_async_copy(info_ref, table_ref, sems.at[3])
    scalars.start()
    lane = lax.broadcasted_iota(jnp.int32, (8, PZ), 1)
    lanes = lane.astype(F32).astype(BF16)
    place = lax.broadcasted_iota(jnp.int32, (PZ, PZ), 0)

    def invert(b, carry):
        first = pl.multiple_of(b * UNROLL, UNROLL)
        dest = dest_ref[pl.ds(first, UNROLL), :]
        moves = jnp.concatenate(
            [jnp.where(place == dest[j : j + 1, :], 1.0, 0.0).astype(BF16) for j in range(UNROLL)], axis=0
        )
        index = lax.dot_general(lanes, moves, (((1,), (1,)), ((), ())), preferred_element_type=F32).astype(jnp.int32)
        for j in range(UNROLL):
            index_ref[first + j] = index[:, PZ * j : PZ * j + PZ]
        return carry

    lax.fori_loop(0, groups // UNROLL, invert, 0)
    loads[1].wait()
    loads[2].wait()
    for b in range(groups // 8):
        here = slice(8 * b, 8 * b + 8)
        cell = cell_ref[here, :]
        rows = [frac_ref[i, here, :] for i in range(3)]
        rows += [(cell >> 10).astype(F32), ((cell >> 7) & (PY - 1)).astype(F32), (cell & (PZ - 1)).astype(F32)]
        for i, values in enumerate(rows):
            load_ref[pl.ds(64 * b + i, 8, stride=8), :] = values
    scalars.wait()

    def append(b, carry):
        rows = []
        for j in range(UNROLL):
            g = b * UNROLL + j
            values = load_ref[pl.ds(pl.multiple_of(g * 8, 8), 8), :]
            ordered = jnp.take_along_axis(values, index_ref[g], axis=1, mode="promise_in_bounds")
            start = 0
            for s in range(slots):
                base = table_ref[s, g]
                offset = base & (PZ - 1)
                rows.append((s, base >> 7, offset, pltpu.roll(ordered, (offset - start) & (PZ - 1), axis=1)))
                start = start + table_ref[slots + s, g]
        for s, at, offset, values in rows:
            pltpu.store(sorted_ref.at[s, at], values, mask=lane >= offset)
            sorted_ref[s, at + 1] = values
        return carry

    lax.fori_loop(0, groups // UNROLL, append, 0)


def fold_rows(values):
    row = lax.broadcasted_iota(jnp.int32, values[0].shape, 0)
    values = list(values) + [jnp.zeros_like(values[0])] * (8 - len(values))
    for step in (1, 2, 4):
        low = (row & step) == 0
        values = [
            jnp.where(low, a, b) + pltpu.roll(jnp.where(low, b, a), step, axis=0)
            for a, b in zip(values[0::2], values[1::2])
        ]
    return values[0]


def sample_slot(s, block_ref, total, sorted_ref, out_ref, table_ref):
    dense = PARTS * PY * DENSE
    width = PY * DENSE
    for c in range(PARTS):
        part = block_ref[c * PX * PY : c * PX * PY + width]
        high = part.astype(BF16)
        low = (part - high.astype(F32)).astype(BF16)
        at = c * width
        for k in range(2):
            table_ref[at : at + width, PZ * k : PZ * k + PZ] = high
            table_ref[dense + at : dense + at + width, PZ * k : PZ * k + PZ] = low
    per = WIDE // PZ
    row = lax.broadcasted_iota(jnp.int32, (PY, PZ), 0).astype(F32)
    depth = lax.broadcasted_iota(jnp.int32, (PZ, WIDE), 0).astype(F32).astype(BF16)

    def in_two(value):
        high = value.astype(BF16).astype(F32)
        return high, value - high

    def packed(value):
        return jnp.broadcast_to(value, (16, WIDE)).astype(BF16)[0:1]

    def step(i, carry):
        loads = [sorted_ref[s, i * per + j] for j in range(per)]
        wide = jnp.concatenate(loads, axis=1)
        along_z, iz = wide[2:3], wide[5:6]
        lower_high, lower_low = in_two(1.0 - along_z)
        upper_high, upper_low = in_two(along_z)
        none = jnp.zeros((), BF16)
        at_lower = depth == packed(iz)
        at_upper = depth == packed(iz + 1.0)
        high = jnp.where(at_lower, packed(lower_high), jnp.where(at_upper, packed(upper_high), none))
        low = jnp.where(at_lower, packed(lower_low), jnp.where(at_upper, packed(upper_low), none))
        product = jnp.dot(table_ref[...], jnp.concatenate([high, low], axis=0), preferred_element_type=F32)
        for j in range(per):
            fx, fy, fz, ix, iy, iz = [jnp.broadcast_to(loads[j][k : k + 1], (PY, PZ)) for k in range(6)]
            lower = jnp.clip(iz.astype(jnp.int32), 0, PZ - 2)
            upper = lower + 1
            weight_y = jnp.where(row == iy, 1.0 - fy, jnp.where(row == iy + 1.0, fy, 0.0))
            lanes = slice(PZ * j, PZ * j + PZ)
            totals = [None] * PARTS
            for x in range(PX):
                weight = weight_y * jnp.where(ix == float(x), 1.0 - fx, jnp.where(ix == float(x - 1), fx, 0.0))
                weight_lower, weight_upper = weight * (1.0 - fz), weight * fz
                for c in range(PARTS):
                    if x < DENSE:
                        at = c * width + x * PY
                        term = (product[at : at + PY, lanes] + product[dense + at : dense + at + PY, lanes]) * weight
                    else:
                        at = (c * PX + x) * PY
                        cells = block_ref[at : at + PY]
                        term = (
                            jnp.take_along_axis(cells, lower, axis=1, mode="promise_in_bounds") * weight_lower
                            + jnp.take_along_axis(cells, upper, axis=1, mode="promise_in_bounds") * weight_upper
                        )
                    totals[c] = term if x == 0 else totals[c] + term
            out_ref[s, i * per + j] = fold_rows(totals)
        return carry

    lax.fori_loop(0, (total + WIDE - 1) // WIDE, step, 0)


def sample_kernel(slots, first, blocks, again, plan_ref, info_ref, sorted_ref, *refs):
    block_refs = refs[:blocks]
    out_ref, table_ref = refs[blocks + again :]
    last = info_ref.shape[1] - 1
    for b in range(blocks):
        s = plan_ref[first + b]

        @pl.when(s >= 0)
        def _():
            total = info_ref[s, last] + info_ref[slots + s, last]
            sample_slot(s, block_refs[b], total, sorted_ref, out_ref, table_ref)


def sample(slots, first, blocks, plan, info, ordered, before):
    again = 0 if before is None else 1
    return kernel_call(
        functools.partial(sample_kernel, slots, first, len(blocks), again),
        jax.ShapeDtypeStruct(ordered.shape, F32),
        [SMEM, SMEM] + [VMEM] * (1 + len(blocks) + again),
        [pltpu.VMEM((2 * PARTS * PY * DENSE, 2 * PZ), BF16)],
        {3 + len(blocks): 0} if again else None,
        cost=2.5 * min(slots, len(blocks)),
    )(plan, info, ordered, *blocks, *([before] if again else []))


def transpose_inverse(matrix):
    cof_00 = matrix[1][1] * matrix[2][2] - matrix[1][2] * matrix[2][1]
    cof_01 = -(matrix[1][0] * matrix[2][2] - matrix[1][2] * matrix[2][0])
    cof_02 = matrix[1][0] * matrix[2][1] - matrix[1][1] * matrix[2][0]
    cof_10 = -(matrix[0][1] * matrix[2][2] - matrix[0][2] * matrix[2][1])
    cof_11 = matrix[0][0] * matrix[2][2] - matrix[0][2] * matrix[2][0]
    cof_12 = -(matrix[0][0] * matrix[2][1] - matrix[0][1] * matrix[2][0])
    cof_20 = matrix[0][1] * matrix[1][2] - matrix[0][2] * matrix[1][1]
    cof_21 = -(matrix[0][0] * matrix[1][2] - matrix[0][2] * matrix[1][0])
    cof_22 = matrix[0][0] * matrix[1][1] - matrix[0][1] * matrix[1][0]
    determinant = matrix[0][0] * cof_00 + matrix[0][1] * cof_01 + matrix[0][2] * cof_02
    reciprocal = 1.0 / determinant
    return [
        [cof_00 * reciprocal, cof_01 * reciprocal, cof_02 * reciprocal],
        [cof_10 * reciprocal, cof_11 * reciprocal, cof_12 * reciprocal],
        [cof_20 * reciprocal, cof_21 * reciprocal, cof_22 * reciprocal],
    ]


def polar_factor(jacobian):
    rotation = jacobian
    for repeat in range(STEPS):
        inverse = transpose_inverse(rotation)
        rotation = [
            [0.5 * (rotation[first][second] + inverse[first][second]) for second in range(3)] for first in range(3)
        ]
    return rotation


def reorient(rotation, components):
    tensor = [
        [components[0], components[3], components[4]],
        [components[3], components[1], components[5]],
        [components[4], components[5], components[2]],
    ]
    left = [
        [
            rotation[first][0] * tensor[0][second]
            + rotation[first][1] * tensor[1][second]
            + rotation[first][2] * tensor[2][second]
            for second in range(3)
        ]
        for first in range(3)
    ]

    def entry(first, second):
        return (
            left[first][0] * rotation[second][0]
            + left[first][1] * rotation[second][1]
            + left[first][2] * rotation[second][2]
        )

    return [entry(0, 0), entry(1, 1), entry(2, 2), entry(0, 1), entry(0, 2), entry(1, 2)]


def pack_kernel(odd_ref, table_ref, field_ref, swap_ref, cross_ref, first_ref, last_ref):
    odd = odd_ref[0] == 1
    cells = table_ref.shape[0]
    half = field_ref.shape[1] // 2
    swap_ref[0:cells, :] = table_ref[...]
    for c in range(3):
        even_rows = field_ref[c, pl.ds(0, half, stride=2), :]
        odd_rows = field_ref[c, pl.ds(1, half, stride=2), :]
        swap_ref[cells + half * c : cells + half * c + half, :] = jnp.where(odd, even_rows, odd_rows)
        cross_ref[half * c : half * c + half, :] = jnp.where(odd, odd_rows, even_rows)
        turned = field_ref[c].T
        first_ref[c : c + 1, :] = turned[0:1]
        last_ref[c : c + 1, :] = turned[PZ - 1 : PZ]


def rotation_kernel(odd_ref, field_ref, swapped_ref, crossed_ref, down_ref, up_ref, out_ref, wide_ref, slope_ref, edge_ref):
    odd = odd_ref[0] == 1
    rows = field_ref.shape[1]
    half = rows // 2
    cells = swapped_ref.shape[0] - 3 * half
    edge_ref[...] = jnp.zeros_like(edge_ref)
    edge_ref[0:3, :] = down_ref[...]
    edge_ref[3:6, :] = up_ref[...]
    edges = edge_ref[...].T
    for c in range(3):
        wide_ref[c, 0:8, :] = jnp.zeros((8, PZ), F32)
        wide_ref[c, 8 : 8 + rows, :] = field_ref[c]
        wide_ref[c, 8 + rows : 16 + rows, :] = jnp.zeros((8, PZ), F32)
        even_rows = wide_ref[c, pl.ds(8, half, stride=2), :]
        odd_rows = wide_ref[c, pl.ds(9, half, stride=2), :]
        paired = swapped_ref[cells + half * c : cells + half * c + half, :]
        other = crossed_ref[half * c : half * c + half, :]
        slope_ref[c, pl.ds(0, half, stride=2), :] = 0.5 * (odd_rows - jnp.where(odd, paired, other))
        slope_ref[c, pl.ds(1, half, stride=2), :] = 0.5 * (jnp.where(odd, other, paired) - even_rows)
    lane = lax.broadcasted_iota(jnp.int32, (16, PZ), 1)
    for b in range(rows // 16):
        jacobian = []
        for c in range(3):
            at = 16 * b
            middle = field_ref[c, at : at + 16, :]
            after = pltpu.roll(middle, PZ - 1, axis=1)
            after = jnp.where(lane == PZ - 1, edges[at : at + 16, 3 + c : 4 + c], after)
            prior = pltpu.roll(middle, 1, axis=1)
            prior = jnp.where(lane == 0, edges[at : at + 16, c : c + 1], prior)
            slopes = [
                slope_ref[c, at : at + 16, :],
                0.5 * (after - prior),
                0.5 * (wide_ref[c, at + 10 : at + 26, :] - wide_ref[c, at + 6 : at + 22, :]),
            ]
            jacobian.append([slopes[d] + 1.0 if d == c else slopes[d] for d in range(3)])
        rotation = polar_factor(jacobian)
        for first in range(3):
            for second in range(3):
                out_ref[3 * first + second, at : at + 16, :] = rotation[first][second]


def along(values, axis, pairs):
    return lax.ppermute(values, axis, pairs)


def both_ways(pairs):
    return list(pairs) + [(b, a) for a, b in pairs]


def finish_kernel(slots, info_ref, slot_ref, pos_ref, samples_ref, rotation_ref, out_hbm, row_ref, out_ref, sems):
    groups = slot_ref.shape[0]
    lane = lax.broadcasted_iota(jnp.int32, (8, PZ), 1)
    stores = []
    for part in range(groups // SHARE):
        for g in range(part * SHARE, part * SHARE + SHARE):
            slot = jnp.broadcast_to(slot_ref[g : g + 1, :], (8, PZ))
            index = jnp.broadcast_to(pos_ref[g : g + 1, :], (8, PZ)) & (PZ - 1)
            result = None
            for s in range(slots):
                base = info_ref[s, g]
                offset, at = base & (PZ - 1), base >> 7
                both = jnp.where(lane >= offset, samples_ref[s, at], samples_ref[s, at + 1])
                value = jnp.take_along_axis(both, index, axis=1, mode="promise_in_bounds")
                result = value if s == 0 else jnp.where(slot == s, value, result)
            row_ref[8 * g : 8 * g + 8, :] = result
        for at in range(part * SHARE, part * SHARE + SHARE, 8):
            components = [row_ref[pl.ds(at * 8 + c, 8, stride=8), :] for c in range(PARTS)]
            rotation = [[rotation_ref[3 * m + n, at : at + 8, :] for n in range(3)] for m in range(3)]
            for c, value in enumerate(reorient(rotation, components)):
                out_ref[c, at : at + 8, :] = value
        here = pl.ds(part * SHARE, SHARE)
        stores.append(pltpu.make_async_copy(out_ref.at[:, here], out_hbm.at[:, here], sems.at[part]))
        stores[-1].start()
    for store in stores:
        store.wait()


def on_device(source, lists, voxel_slot, voxel_cell, frac, displace):
    count = lax.axis_size("bx")
    columns = lax.axis_size("by")
    row = lax.axis_index("bx")
    lines = count // 2
    slots = lists.shape[2]
    voxels = voxel_cell.shape[2]
    groups = voxels // PZ
    half = groups // 2
    cells = PARTS * PX * PY
    table = source.reshape(cells, PZ)
    field = displace.reshape(3, groups, PZ)
    odd = (row % 2).astype(jnp.int32).reshape(1)

    swap = [(i, i ^ 1) for i in range(count)]
    forward = [(i, (i + 2) % count) for i in range(count)]
    backward = [(b, a) for a, b in forward]
    line = jax.ShapeDtypeStruct((3, groups), F32)
    packed, facing, first_lane, last_lane = kernel_call(
        pack_kernel,
        (
            jax.ShapeDtypeStruct((cells + 3 * half, PZ), F32),
            jax.ShapeDtypeStruct((3 * half, PZ), F32),
            line,
            line,
        ),
        [SMEM, VMEM, VMEM],
    )(odd, table, field)
    crossed = along(facing, "bx", both_ways([(i, i + 1) for i in range(1, count - 1, 2)]))
    down = along(last_lane, "by", [(i, i + 1) for i in range(columns - 1)])
    up = along(first_lane, "by", [(i + 1, i) for i in range(columns - 1)])
    slot_rows = voxel_slot.reshape(groups, PZ)
    sent = table
    swapped = along(packed, "bx", swap)
    ahead = along(sent, "bx", forward)
    behind = along(sent, "bx", backward)

    ints = functools.partial(jax.ShapeDtypeStruct, dtype=jnp.int32)
    ordered, pos, info = kernel_call(
        functools.partial(order_kernel, slots),
        (
            jax.ShapeDtypeStruct((slots, groups + WIDE // PZ + 1, 8, PZ), F32),
            ints((groups, PZ)),
            ints((2 * slots, groups)),
        ),
        [HBM] * 3,
        [
            pltpu.VMEM((groups, PZ), jnp.int32),
            pltpu.VMEM((groups, PZ), jnp.int32),
            pltpu.VMEM((3, groups, PZ), F32),
            pltpu.VMEM((groups, PZ), jnp.int32),
            pltpu.VMEM((groups * 8, PZ), F32),
            pltpu.VMEM((groups, 8, PZ), jnp.int32),
            pltpu.SMEM((2 * slots, groups), jnp.int32),
            pltpu.SemaphoreType.DMA((4,)),
        ],
        cost=7.0,
    )(*[
        pltpu.with_memory_space_constraint(a, pltpu.HBM)
        for a in (slot_rows, voxel_cell.reshape(groups, PZ), frac.reshape(3, groups, PZ))
    ])
    ahead, behind, swapped, ordered = lax.optimization_barrier((ahead, behind, swapped, ordered))

    steps = [[m for m in (k, -k) if 2 * m > -lines] for k in range(1, lines // 2 + 1)]
    places = [(0, 0), (0, 1)] + [(m, over) for step in steps for over in (0, 1) for m in step]
    my_slabs = lax.dynamic_index_in_dim(lists[:, 0, :], row, 0, keepdims=False)
    far = jnp.array([k for k, _ in places], jnp.int32)
    over = jnp.array([k for _, k in places], jnp.int32)
    owners = ((row // 2 - far + count) % lines) * 2 + (row % 2 + over) % 2
    listed = owners[:, None] == my_slabs[None, :]
    plan = jnp.max(jnp.where(listed, jnp.arange(slots, dtype=jnp.int32)[None, :], -1), axis=1)

    blocks = [table, swapped]
    for k in range(1, lines // 2 + 1):
        new = [ahead] + ([behind] if 2 * k < lines else [])
        blocks += new + [along(block, "bx", swap) for block in new]
        if 2 * (k + 1) <= lines:
            ahead = along(ahead, "bx", forward)
        if 2 * (k + 1) < lines:
            behind = along(behind, "bx", backward)
    samples = sample(slots, 0, blocks[:4], plan, info, ordered, None)
    samples = sample(slots, 4, blocks[4:-1], plan, info, ordered, samples)
    samples = sample(slots, count - 1, blocks[-1:], plan, info, ordered, samples)

    rotation = kernel_call(
        rotation_kernel,
        jax.ShapeDtypeStruct((9, groups, PZ), F32),
        [SMEM] + [VMEM] * 5,
        [
            pltpu.VMEM((3, groups + 16, PZ), F32),
            pltpu.VMEM((3, groups, PZ), F32),
            pltpu.VMEM((8, groups), F32),
        ],
    )(odd, field, swapped, crossed, down, up)

    result = kernel_call(
        functools.partial(finish_kernel, slots),
        jax.ShapeDtypeStruct((PARTS, groups, PZ), F32),
        [SMEM] + [VMEM] * 4,
        [
            pltpu.VMEM((groups * 8, PZ), F32),
            pltpu.VMEM((PARTS, groups, PZ), F32),
            pltpu.SemaphoreType.DMA((groups // SHARE,)),
        ],
        out_spec=HBM,
    )(info, slot_rows, pos, samples, rotation)
    return result.reshape(1, 1, PARTS, voxels)


def solution(mesh):
    return jax.shard_map(
        on_device,
        mesh=mesh,
        in_specs=(
            P("bx", "by", None, None),
            P(None, "by", None),
            P("bx", "by", None),
            P("bx", "by", None),
            P("bx", "by", None, None),
            P(None, None, "bx", "by"),
        ),
        out_specs=P("bx", "by", None, None),
        check_vma=False,
    )
```

```python
import functools

import jax
import jax.numpy as jnp
from jax import lax
from jax.experimental import pallas as pl
from jax.experimental.pallas import tpu as pltpu
from jax.sharding import PartitionSpec as P

PX = 8
PY = 8
PZ = 128
STEPS = 2
PARTS = 6
DENSE = 6
WIDE = 1024
UNROLL = 16
SHARE = 32
F32 = jnp.float32
BF16 = jnp.bfloat16
VMEM = pl.BlockSpec(memory_space=pltpu.VMEM)
SMEM = pl.BlockSpec(memory_space=pltpu.SMEM)
HBM = pl.BlockSpec(memory_space=pltpu.HBM)


def kernel_call(body, outs, ins, scratch=(), aliases=None, cost=1.0, out_spec=VMEM):
    return pl.pallas_call(
        body,
        out_shape=outs,
        in_specs=ins,
        out_specs=jax.tree.map(lambda _: out_spec, outs),
        scratch_shapes=list(scratch),
        input_output_aliases=aliases or {},
        cost_estimate=pl.CostEstimate(flops=0, bytes_accessed=int(cost * 3.0e6), transcendentals=0),
        compiler_params=pltpu.CompilerParams(vmem_limit_bytes=24 * 2**20),
    )


def ranks(slots, slot, pos_ref, dest_ref, info_ref):
    groups = slot.shape[0]
    row = lax.broadcasted_iota(jnp.int32, (PZ, PZ), 0)
    col = lax.broadcasted_iota(jnp.int32, (PZ, PZ), 1)
    before = jnp.where(row < col, 1.0, 0.0).astype(BF16)
    grow = lax.broadcasted_iota(jnp.int32, (groups, groups), 0)
    gcol = lax.broadcasted_iota(jnp.int32, (groups, groups), 1)
    gbefore = jnp.where(grow < gcol, 1.0, 0.0).astype(BF16)
    gafter = jnp.where(grow > gcol, 1.0, 0.0).astype(BF16)
    ones = jnp.ones((PZ, PZ), BF16)
    dest = jnp.zeros((groups, PZ), F32)
    pos = jnp.zeros((groups, PZ), F32)
    start = jnp.zeros((groups, PZ), F32)
    for s in range(slots):
        on = slot == s
        mask = jnp.where(on, 1.0, 0.0).astype(BF16)
        rank = jnp.dot(mask, before, preferred_element_type=F32)
        count = jnp.dot(mask, ones, preferred_element_type=F32)
        base = jnp.dot(gafter, count.astype(BF16), preferred_element_type=F32)
        dest = jnp.where(on, rank + start, dest)
        pos = jnp.where(on, rank + base, pos)
        start = start + count
        across = lax.dot_general(ones[:PY], mask, (((1,), (1,)), ((), ())), preferred_element_type=F32)
        ahead = jnp.dot(across.astype(BF16), gbefore, preferred_element_type=F32)
        info_ref[s : s + 1, :] = ahead[0:1].astype(jnp.int32)
        info_ref[slots + s : slots + s + 1, :] = across[0:1].astype(jnp.int32)
    pos_ref[...] = pos.astype(jnp.int32)
    dest_ref[...] = dest.astype(jnp.int32)


def order_kernel(
    slots, slot_hbm, cell_hbm, frac_hbm, sorted_ref, pos_ref, info_ref,
    slot_ref, cell_ref, frac_ref, dest_ref, load_ref, index_ref, table_ref, sems,
):
    groups = pos_ref.shape[0]
    loads = [
        pltpu.make_async_copy(slot_hbm, slot_ref, sems.at[0]),
        pltpu.make_async_copy(cell_hbm, cell_ref, sems.at[1]),
        pltpu.make_async_copy(frac_hbm, frac_ref, sems.at[2]),
    ]
    for load in loads:
        load.start()
    loads[0].wait()
    ranks(slots, slot_ref[...], pos_ref, dest_ref, info_ref)
    scalars = pltpu.make_async_copy(info_ref, table_ref, sems.at[3])
    scalars.start()
    lane = lax.broadcasted_iota(jnp.int32, (8, PZ), 1)
    lanes = lane.astype(F32).astype(BF16)
    place = lax.broadcasted_iota(jnp.int32, (PZ, PZ), 0)

    def invert(b, carry):
        first = pl.multiple_of(b * UNROLL, UNROLL)
        dest = dest_ref[pl.ds(first, UNROLL), :]
        moves = jnp.concatenate(
            [jnp.where(place == dest[j : j + 1, :], 1.0, 0.0).astype(BF16) for j in range(UNROLL)], axis=0
        )
        index = lax.dot_general(lanes, moves, (((1,), (1,)), ((), ())), preferred_element_type=F32).astype(jnp.int32)
        for j in range(UNROLL):
            index_ref[first + j] = index[:, PZ * j : PZ * j + PZ]
        return carry

    lax.fori_loop(0, groups // UNROLL, invert, 0)
    loads[1].wait()
    loads[2].wait()
    for b in range(groups // 8):
        here = slice(8 * b, 8 * b + 8)
        cell = cell_ref[here, :]
        rows = [frac_ref[i, here, :] for i in range(3)]
        rows += [(cell >> 10).astype(F32), ((cell >> 7) & (PY - 1)).astype(F32), (cell & (PZ - 1)).astype(F32)]
        for i, values in enumerate(rows):
            load_ref[pl.ds(64 * b + i, 8, stride=8), :] = values
    scalars.wait()

    def append(b, carry):
        rows = []
        for j in range(UNROLL):
            g = b * UNROLL + j
            values = load_ref[pl.ds(pl.multiple_of(g * 8, 8), 8), :]
            ordered = jnp.take_along_axis(values, index_ref[g], axis=1, mode="promise_in_bounds")
            start = 0
            for s in range(slots):
                base = table_ref[s, g]
                offset = base & (PZ - 1)
                rows.append((s, base >> 7, offset, pltpu.roll(ordered, (offset - start) & (PZ - 1), axis=1)))
                start = start + table_ref[slots + s, g]
        for s, at, offset, values in rows:
            pltpu.store(sorted_ref.at[s, at], values, mask=lane >= offset)
            sorted_ref[s, at + 1] = values
        return carry

    lax.fori_loop(0, groups // UNROLL, append, 0)


def fold_rows(values):
    row = lax.broadcasted_iota(jnp.int32, values[0].shape, 0)
    values = list(values) + [jnp.zeros_like(values[0])] * (8 - len(values))
    for step in (1, 2, 4):
        low = (row & step) == 0
        values = [
            jnp.where(low, a, b) + pltpu.roll(jnp.where(low, b, a), step, axis=0)
            for a, b in zip(values[0::2], values[1::2])
        ]
    return values[0]


def sample_slot(s, block_ref, total, sorted_ref, out_ref, table_ref):
    dense = PARTS * PY * DENSE
    width = PY * DENSE
    for c in range(PARTS):
        part = block_ref[c * PX * PY : c * PX * PY + width]
        high = part.astype(BF16)
        low = (part - high.astype(F32)).astype(BF16)
        at = c * width
        for k in range(2):
            table_ref[at : at + width, PZ * k : PZ * k + PZ] = high
            table_ref[dense + at : dense + at + width, PZ * k : PZ * k + PZ] = low
    per = WIDE // PZ
    row = lax.broadcasted_iota(jnp.int32, (PY, PZ), 0).astype(F32)
    depth = lax.broadcasted_iota(jnp.int32, (PZ, WIDE), 0).astype(F32).astype(BF16)

    def in_two(value):
        high = value.astype(BF16).astype(F32)
        return high, value - high

    def packed(value):
        return jnp.broadcast_to(value, (16, WIDE)).astype(BF16)[0:1]

    def step(i, carry):
        loads = [sorted_ref[s, i * per + j] for j in range(per)]
        wide = jnp.concatenate(loads, axis=1)
        along_z, iz = wide[2:3], wide[5:6]
        lower_high, lower_low = in_two(1.0 - along_z)
        upper_high, upper_low = in_two(along_z)
        none = jnp.zeros((), BF16)
        at_lower = depth == packed(iz)
        at_upper = depth == packed(iz + 1.0)
        high = jnp.where(at_lower, packed(lower_high), jnp.where(at_upper, packed(upper_high), none))
        low = jnp.where(at_lower, packed(lower_low), jnp.where(at_upper, packed(upper_low), none))
        product = jnp.dot(table_ref[...], jnp.concatenate([high, low], axis=0), preferred_element_type=F32)
        for j in range(per):
            fx, fy, fz, ix, iy, iz = [jnp.broadcast_to(loads[j][k : k + 1], (PY, PZ)) for k in range(6)]
            lower = jnp.clip(iz.astype(jnp.int32), 0, PZ - 2)
            upper = lower + 1
            weight_y = jnp.where(row == iy, 1.0 - fy, jnp.where(row == iy + 1.0, fy, 0.0))
            lanes = slice(PZ * j, PZ * j + PZ)
            totals = [None] * PARTS
            for x in range(PX):
                weight = weight_y * jnp.where(ix == float(x), 1.0 - fx, jnp.where(ix == float(x - 1), fx, 0.0))
                weight_lower, weight_upper = weight * (1.0 - fz), weight * fz
                for c in range(PARTS):
                    if x < DENSE:
                        at = c * width + x * PY
                        term = (product[at : at + PY, lanes] + product[dense + at : dense + at + PY, lanes]) * weight
                    else:
                        at = (c * PX + x) * PY
                        cells = block_ref[at : at + PY]
                        term = (
                            jnp.take_along_axis(cells, lower, axis=1, mode="promise_in_bounds") * weight_lower
                            + jnp.take_along_axis(cells, upper, axis=1, mode="promise_in_bounds") * weight_upper
                        )
                    totals[c] = term if x == 0 else totals[c] + term
            out_ref[s, i * per + j] = fold_rows(totals)
        return carry

    lax.fori_loop(0, (total + WIDE - 1) // WIDE, step, 0)


def sample_kernel(slots, lines, places, part, lead, blocks, again, row_ref, slab_ref, info_ref, sorted_ref, *refs):
    block_refs = refs[:blocks]
    out_ref, table_ref = refs[blocks + again :]
    last = info_ref.shape[1] - 1
    row = row_ref[0]
    found = jnp.int32(0)
    for b, (distance, over) in enumerate(places):
        owner = lax.rem(row // 2 + (lines - distance), lines) * 2 + lax.rem(row + over, 2)
        s = jnp.int32(-1)
        for k in range(slots):
            s = jnp.where(slab_ref[k] == owner, k, s)
        take = s >= 0
        if b < lead:
            is_lead = jnp.logical_and(take, found == 0)
            found = jnp.where(take, 1, found)
            take = is_lead if part is None else jnp.logical_and(take, jnp.logical_not(is_lead))
        at = b if part is None else b - part[0]
        if not 0 <= at < blocks:
            continue

        @pl.when(take)
        def _(s=s, at=at):
            total = info_ref[s, last] + info_ref[slots + s, last]
            sample_slot(s, block_refs[at], total, sorted_ref, out_ref, table_ref)


def sample(setting, part, blocks, row, slabs, info, ordered, before):
    again = 0 if before is None else 1
    return kernel_call(
        functools.partial(sample_kernel, *setting[:3], part, setting[3], len(blocks), again),
        jax.ShapeDtypeStruct(ordered.shape, F32),
        [SMEM] * 3 + [VMEM] * (1 + len(blocks) + again),
        [pltpu.VMEM((2 * PARTS * PY * DENSE, 2 * PZ), BF16)],
        {4 + len(blocks): 0} if again else None,
        cost=2.5 if part is None else 5.0,
    )(row, slabs, info, ordered, *blocks, *([before] if again else []))


def transpose_inverse(matrix):
    cof_00 = matrix[1][1] * matrix[2][2] - matrix[1][2] * matrix[2][1]
    cof_01 = -(matrix[1][0] * matrix[2][2] - matrix[1][2] * matrix[2][0])
    cof_02 = matrix[1][0] * matrix[2][1] - matrix[1][1] * matrix[2][0]
    cof_10 = -(matrix[0][1] * matrix[2][2] - matrix[0][2] * matrix[2][1])
    cof_11 = matrix[0][0] * matrix[2][2] - matrix[0][2] * matrix[2][0]
    cof_12 = -(matrix[0][0] * matrix[2][1] - matrix[0][1] * matrix[2][0])
    cof_20 = matrix[0][1] * matrix[1][2] - matrix[0][2] * matrix[1][1]
    cof_21 = -(matrix[0][0] * matrix[1][2] - matrix[0][2] * matrix[1][0])
    cof_22 = matrix[0][0] * matrix[1][1] - matrix[0][1] * matrix[1][0]
    determinant = matrix[0][0] * cof_00 + matrix[0][1] * cof_01 + matrix[0][2] * cof_02
    reciprocal = 1.0 / determinant
    return [
        [cof_00 * reciprocal, cof_01 * reciprocal, cof_02 * reciprocal],
        [cof_10 * reciprocal, cof_11 * reciprocal, cof_12 * reciprocal],
        [cof_20 * reciprocal, cof_21 * reciprocal, cof_22 * reciprocal],
    ]


def polar_factor(jacobian):
    rotation = jacobian
    for repeat in range(STEPS):
        inverse = transpose_inverse(rotation)
        rotation = [
            [0.5 * (rotation[first][second] + inverse[first][second]) for second in range(3)] for first in range(3)
        ]
    return rotation


def reorient(rotation, components):
    tensor = [
        [components[0], components[3], components[4]],
        [components[3], components[1], components[5]],
        [components[4], components[5], components[2]],
    ]
    left = [
        [
            rotation[first][0] * tensor[0][second]
            + rotation[first][1] * tensor[1][second]
            + rotation[first][2] * tensor[2][second]
            for second in range(3)
        ]
        for first in range(3)
    ]

    def entry(first, second):
        return (
            left[first][0] * rotation[second][0]
            + left[first][1] * rotation[second][1]
            + left[first][2] * rotation[second][2]
        )

    return [entry(0, 0), entry(1, 1), entry(2, 2), entry(0, 1), entry(0, 2), entry(1, 2)]


def pack_kernel(place_ref, table_hbm, field_hbm, swap_ref, cross_ref, near_ref, far_ref, field_ref, sems):
    odd = (place_ref[0] & 1) == 1
    odd_column = (place_ref[1] & 1) == 1
    cells = table_hbm.shape[0]
    half = field_ref.shape[1] // 2
    load_field = pltpu.make_async_copy(field_hbm, field_ref, sems.at[0])
    load_table = pltpu.make_async_copy(table_hbm, swap_ref.at[0:cells], sems.at[1])
    load_field.start()
    load_table.start()
    load_field.wait()
    for c in range(3):
        even_rows = field_ref[c, pl.ds(0, half, stride=2), :]
        odd_rows = field_ref[c, pl.ds(1, half, stride=2), :]
        swap_ref[cells + half * c : cells + half * c + half, :] = jnp.where(odd, even_rows, odd_rows)
        cross_ref[half * c : half * c + half, :] = jnp.where(odd, odd_rows, even_rows)
        turned = field_ref[c].T
        first, last = turned[0:1], turned[PZ - 1 : PZ]
        near_ref[c : c + 1, :] = jnp.where(odd_column, first, last)
        far_ref[c : c + 1, :] = jnp.where(odd_column, last, first)
    load_table.wait()


def rotation_kernel(place_ref, field_ref, swapped_ref, crossed_ref, near_ref, far_ref, out_ref, wide_ref, slope_ref, edge_ref):
    odd = (place_ref[0] & 1) == 1
    odd_column = (place_ref[1] & 1) == 1
    rows = field_ref.shape[1]
    half = rows // 2
    cells = swapped_ref.shape[0] - 3 * half
    edge_ref[...] = jnp.zeros_like(edge_ref)
    edge_ref[0:3, :] = jnp.where(odd_column, near_ref[...], far_ref[...])
    edge_ref[3:6, :] = jnp.where(odd_column, far_ref[...], near_ref[...])
    edges = edge_ref[...].T
    for c in range(3):
        wide_ref[c, 0:8, :] = jnp.zeros((8, PZ), F32)
        wide_ref[c, 8 : 8 + rows, :] = field_ref[c]
        wide_ref[c, 8 + rows : 16 + rows, :] = jnp.zeros((8, PZ), F32)
        even_rows = wide_ref[c, pl.ds(8, half, stride=2), :]
        odd_rows = wide_ref[c, pl.ds(9, half, stride=2), :]
        paired = swapped_ref[cells + half * c : cells + half * c + half, :]
        other = crossed_ref[half * c : half * c + half, :]
        slope_ref[c, pl.ds(0, half, stride=2), :] = 0.5 * (odd_rows - jnp.where(odd, paired, other))
        slope_ref[c, pl.ds(1, half, stride=2), :] = 0.5 * (jnp.where(odd, other, paired) - even_rows)
    lane = lax.broadcasted_iota(jnp.int32, (16, PZ), 1)
    for b in range(rows // 16):
        jacobian = []
        for c in range(3):
            at = 16 * b
            middle = field_ref[c, at : at + 16, :]
            after = pltpu.roll(middle, PZ - 1, axis=1)
            after = jnp.where(lane == PZ - 1, edges[at : at + 16, 3 + c : 4 + c], after)
            prior = pltpu.roll(middle, 1, axis=1)
            prior = jnp.where(lane == 0, edges[at : at + 16, c : c + 1], prior)
            slopes = [
                slope_ref[c, at : at + 16, :],
                0.5 * (after - prior),
                0.5 * (wide_ref[c, at + 10 : at + 26, :] - wide_ref[c, at + 6 : at + 22, :]),
            ]
            jacobian.append([slopes[d] + 1.0 if d == c else slopes[d] for d in range(3)])
        rotation = polar_factor(jacobian)
        for first in range(3):
            for second in range(3):
                out_ref[3 * first + second, at : at + 16, :] = rotation[first][second]


def along(values, axis, pairs):
    return lax.ppermute(values, axis, pairs)


def both_ways(pairs):
    return list(pairs) + [(b, a) for a, b in pairs]


def finish_kernel(slots, info_ref, slot_ref, pos_ref, samples_ref, rotation_ref, out_hbm, row_ref, out_ref, sems):
    groups = slot_ref.shape[0]
    lane = lax.broadcasted_iota(jnp.int32, (8, PZ), 1)
    stores = []
    for part in range(groups // SHARE):
        for g in range(part * SHARE, part * SHARE + SHARE):
            slot = jnp.broadcast_to(slot_ref[g : g + 1, :], (8, PZ))
            index = jnp.broadcast_to(pos_ref[g : g + 1, :], (8, PZ)) & (PZ - 1)
            result = None
            for s in range(slots):
                base = info_ref[s, g]
                offset, at = base & (PZ - 1), base >> 7
                both = jnp.where(lane >= offset, samples_ref[s, at], samples_ref[s, at + 1])
                value = jnp.take_along_axis(both, index, axis=1, mode="promise_in_bounds")
                result = value if s == 0 else jnp.where(slot == s, value, result)
            row_ref[8 * g : 8 * g + 8, :] = result
        for at in range(part * SHARE, part * SHARE + SHARE, 8):
            components = [row_ref[pl.ds(at * 8 + c, 8, stride=8), :] for c in range(PARTS)]
            rotation = [[rotation_ref[3 * m + n, at : at + 8, :] for n in range(3)] for m in range(3)]
            for c, value in enumerate(reorient(rotation, components)):
                out_ref[c, at : at + 8, :] = value
        here = pl.ds(part * SHARE, SHARE)
        stores.append(pltpu.make_async_copy(out_ref.at[:, here], out_hbm.at[:, here], sems.at[part]))
        stores[-1].start()
    for store in stores:
        store.wait()


def on_device(source, lists, voxel_slot, voxel_cell, frac, displace):
    count = lax.axis_size("bx")
    columns = lax.axis_size("by")
    row = lax.axis_index("bx")
    lines = count // 2
    slots = lists.shape[2]
    voxels = voxel_cell.shape[2]
    groups = voxels // PZ
    half = groups // 2
    cells = PARTS * PX * PY
    table = source.reshape(cells, PZ)
    field = displace.reshape(3, groups, PZ)
    here = jnp.stack([row, lax.axis_index("by")]).astype(jnp.int32)

    swap = [(i, i ^ 1) for i in range(count)]
    forward = [(i, (i + 2) % count) for i in range(count)]
    backward = [(b, a) for a, b in forward]
    line = jax.ShapeDtypeStruct((3, groups), F32)
    packed, facing, near_lane, far_lane = kernel_call(
        pack_kernel,
        (
            jax.ShapeDtypeStruct((cells + 3 * half, PZ), F32),
            jax.ShapeDtypeStruct((3 * half, PZ), F32),
            line,
            line,
        ),
        [SMEM, HBM, HBM],
        [pltpu.VMEM((3, groups, PZ), F32), pltpu.SemaphoreType.DMA((2,))],
    )(here, *[pltpu.with_memory_space_constraint(a, pltpu.HBM) for a in (table, field)])
    slot_rows = voxel_slot.reshape(groups, PZ)
    sent = table
    swapped = along(packed, "bx", swap)
    near = along(near_lane, "by", both_ways([(i, i + 1) for i in range(0, columns - 1, 2)]))
    far = along(far_lane, "by", both_ways([(i, i + 1) for i in range(1, columns - 1, 2)]))
    ahead = along(sent, "bx", forward)
    behind = along(sent, "bx", backward)

    ints = functools.partial(jax.ShapeDtypeStruct, dtype=jnp.int32)
    ordered, pos, info = kernel_call(
        functools.partial(order_kernel, slots),
        (
            jax.ShapeDtypeStruct((slots, groups + WIDE // PZ + 1, 8, PZ), F32),
            ints((groups, PZ)),
            ints((2 * slots, groups)),
        ),
        [HBM] * 3,
        [
            pltpu.VMEM((groups, PZ), jnp.int32),
            pltpu.VMEM((groups, PZ), jnp.int32),
            pltpu.VMEM((3, groups, PZ), F32),
            pltpu.VMEM((groups, PZ), jnp.int32),
            pltpu.VMEM((groups * 8, PZ), F32),
            pltpu.VMEM((groups, 8, PZ), jnp.int32),
            pltpu.SMEM((2 * slots, groups), jnp.int32),
            pltpu.SemaphoreType.DMA((4,)),
        ],
        cost=7.0,
    )(*[
        pltpu.with_memory_space_constraint(a, pltpu.HBM)
        for a in (slot_rows, voxel_cell.reshape(groups, PZ), frac.reshape(3, groups, PZ))
    ])
    facing, swapped, ordered = lax.optimization_barrier((facing, swapped, ordered))
    crossed = along(facing, "bx", both_ways([(i, i + 1) for i in range(1, count - 1, 2)]))
    ahead, behind, near_lane, far_lane, ordered = lax.optimization_barrier((ahead, behind, near, far, ordered))

    near = {1: ahead}
    if lines > 2:
        near[-1] = behind
    far = {}
    for k in range(2, lines // 2 + 1):
        far[k] = ahead = along(ahead, "bx", forward)
        if 2 * k < lines:
            far[-k] = behind = along(behind, "bx", backward)
    near_over = {k: along(block, "bx", swap) for k, block in near.items()}

    my_slabs = lax.dynamic_index_in_dim(lists[:, 0, :], row, 0, keepdims=False)
    places = [(0, 0), (0, 1)] + [(k, 0) for k in (*near, *far)] + [(k, 1) for k in (*near, *far)]
    blocks = [packed, swapped, *near.values()]
    setting = (slots, lines, places, len(blocks))
    samples = sample(setting, None, blocks, here, my_slabs, info, ordered, None)
    if far:
        *later, samples = lax.optimization_barrier((*far.values(), samples))
        far = dict(zip(far, later))
    far_over = {k: along(block, "bx", swap) for k, block in far.items()}
    blocks += far.values()
    samples = sample(setting, (0, len(blocks)), blocks, here, my_slabs, info, ordered, samples)
    for over in (near_over, far_over):
        first = len(blocks)
        blocks += over.values()
        if over:
            samples = sample(setting, (first, len(blocks)), [*over.values()], here, my_slabs, info, ordered, samples)
        if over is near_over:
            crossed, samples = lax.optimization_barrier((crossed, samples))

    rotation = kernel_call(
        rotation_kernel,
        jax.ShapeDtypeStruct((9, groups, PZ), F32),
        [SMEM] + [VMEM] * 5,
        [
            pltpu.VMEM((3, groups + 16, PZ), F32),
            pltpu.VMEM((3, groups, PZ), F32),
            pltpu.VMEM((8, groups), F32),
        ],
    )(here, field, swapped, crossed, near_lane, far_lane)

    result = kernel_call(
        functools.partial(finish_kernel, slots),
        jax.ShapeDtypeStruct((PARTS, groups, PZ), F32),
        [SMEM] + [VMEM] * 4,
        [
            pltpu.VMEM((groups * 8, PZ), F32),
            pltpu.VMEM((PARTS, groups, PZ), F32),
            pltpu.SemaphoreType.DMA((groups // SHARE,)),
        ],
        out_spec=HBM,
    )(info, slot_rows, pos, samples, rotation)
    return result.reshape(1, 1, PARTS, voxels)


def solution(mesh):
    return jax.shard_map(
        on_device,
        mesh=mesh,
        in_specs=(
            P("bx", "by", None, None),
            P(None, "by", None),
            P("bx", "by", None),
            P("bx", "by", None),
            P("bx", "by", None, None),
            P(None, None, "bx", "by"),
        ),
        out_specs=P("bx", "by", None, None),
        check_vma=False,
    )
```

```python
import functools

import jax
import jax.numpy as jnp
from jax import lax
from jax.experimental import pallas as pl
from jax.experimental.pallas import tpu as pltpu
from jax.sharding import PartitionSpec as P

PX = 8
PY = 8
PZ = 128
STEPS = 2
PARTS = 6
DENSE = 6
WIDE = 1408
UNROLL = 16
SHARE = 32
F32 = jnp.float32
BF16 = jnp.bfloat16
VMEM = pl.BlockSpec(memory_space=pltpu.VMEM)
SMEM = pl.BlockSpec(memory_space=pltpu.SMEM)
HBM = pl.BlockSpec(memory_space=pltpu.HBM)


def kernel_call(body, outs, ins, scratch=(), aliases=None, cost=1.0, out_spec=VMEM):
    return pl.pallas_call(
        body,
        out_shape=outs,
        in_specs=ins,
        out_specs=jax.tree.map(lambda _: out_spec, outs),
        scratch_shapes=list(scratch),
        input_output_aliases=aliases or {},
        cost_estimate=pl.CostEstimate(flops=0, bytes_accessed=int(cost * 3.0e6), transcendentals=0),
        compiler_params=pltpu.CompilerParams(vmem_limit_bytes=24 * 2**20),
    )


def ranks(slots, slot, pos_ref, dest_ref, info_ref):
    groups = slot.shape[0]
    row = lax.broadcasted_iota(jnp.int32, (PZ, PZ), 0)
    col = lax.broadcasted_iota(jnp.int32, (PZ, PZ), 1)
    before = jnp.where(row < col, 1.0, 0.0).astype(BF16)
    grow = lax.broadcasted_iota(jnp.int32, (groups, groups), 0)
    gcol = lax.broadcasted_iota(jnp.int32, (groups, groups), 1)
    gbefore = jnp.where(grow < gcol, 1.0, 0.0).astype(BF16)
    gafter = jnp.where(grow > gcol, 1.0, 0.0).astype(BF16)
    ones = jnp.ones((PZ, PZ), BF16)
    dest = jnp.zeros((groups, PZ), F32)
    pos = jnp.zeros((groups, PZ), F32)
    start = jnp.zeros((groups, PZ), F32)
    for s in range(slots):
        on = slot == s
        mask = jnp.where(on, 1.0, 0.0).astype(BF16)
        rank = jnp.dot(mask, before, preferred_element_type=F32)
        count = jnp.dot(mask, ones, preferred_element_type=F32)
        base = jnp.dot(gafter, count.astype(BF16), preferred_element_type=F32)
        dest = jnp.where(on, rank + start, dest)
        pos = jnp.where(on, rank + base, pos)
        start = start + count
        across = lax.dot_general(ones[:PY], mask, (((1,), (1,)), ((), ())), preferred_element_type=F32)
        ahead = jnp.dot(across.astype(BF16), gbefore, preferred_element_type=F32)
        info_ref[s : s + 1, :] = ahead[0:1].astype(jnp.int32)
        info_ref[slots + s : slots + s + 1, :] = across[0:1].astype(jnp.int32)
    pos_ref[...] = pos.astype(jnp.int32)
    dest_ref[...] = dest.astype(jnp.int32)


def order_kernel(
    slots, slot_hbm, cell_hbm, frac_hbm, sorted_ref, pos_ref, info_ref,
    slot_ref, cell_ref, frac_ref, dest_ref, load_ref, index_ref, table_ref, sems,
):
    groups = pos_ref.shape[0]
    loads = [
        pltpu.make_async_copy(slot_hbm, slot_ref, sems.at[0]),
        pltpu.make_async_copy(cell_hbm, cell_ref, sems.at[1]),
        pltpu.make_async_copy(frac_hbm, frac_ref, sems.at[2]),
    ]
    for load in loads:
        load.start()
    loads[0].wait()
    ranks(slots, slot_ref[...], pos_ref, dest_ref, info_ref)
    scalars = pltpu.make_async_copy(info_ref, table_ref, sems.at[3])
    scalars.start()
    lane = lax.broadcasted_iota(jnp.int32, (8, PZ), 1)
    lanes = lane.astype(F32).astype(BF16)
    place = lax.broadcasted_iota(jnp.int32, (PZ, PZ), 0)

    def invert(b, carry):
        first = pl.multiple_of(b * UNROLL, UNROLL)
        dest = dest_ref[pl.ds(first, UNROLL), :]
        moves = jnp.concatenate(
            [jnp.where(place == dest[j : j + 1, :], 1.0, 0.0).astype(BF16) for j in range(UNROLL)], axis=0
        )
        index = lax.dot_general(lanes, moves, (((1,), (1,)), ((), ())), preferred_element_type=F32).astype(jnp.int32)
        for j in range(UNROLL):
            index_ref[first + j] = index[:, PZ * j : PZ * j + PZ]
        return carry

    lax.fori_loop(0, groups // UNROLL, invert, 0)
    loads[1].wait()
    loads[2].wait()
    for b in range(groups // 8):
        here = slice(8 * b, 8 * b + 8)
        cell = cell_ref[here, :]
        rows = [frac_ref[i, here, :] for i in range(3)]
        rows += [(cell >> 10).astype(F32), ((cell >> 7) & (PY - 1)).astype(F32), (cell & (PZ - 1)).astype(F32)]
        for i, values in enumerate(rows):
            load_ref[pl.ds(64 * b + i, 8, stride=8), :] = values
    scalars.wait()

    def append(b, carry):
        rows = []
        for j in range(UNROLL):
            g = b * UNROLL + j
            values = load_ref[pl.ds(pl.multiple_of(g * 8, 8), 8), :]
            ordered = jnp.take_along_axis(values, index_ref[g], axis=1, mode="promise_in_bounds")
            start = 0
            for s in range(slots):
                base = table_ref[s, g]
                offset = base & (PZ - 1)
                rows.append((s, base >> 7, offset, pltpu.roll(ordered, (offset - start) & (PZ - 1), axis=1)))
                start = start + table_ref[slots + s, g]
        for s, at, offset, values in rows:
            pltpu.store(sorted_ref.at[s, at], values, mask=lane >= offset)
            sorted_ref[s, at + 1] = values
        return carry

    lax.fori_loop(0, groups // UNROLL, append, 0)


def fold_rows(values):
    row = lax.broadcasted_iota(jnp.int32, values[0].shape, 0)
    values = list(values) + [jnp.zeros_like(values[0])] * (8 - len(values))
    for step in (1, 2, 4):
        low = (row & step) == 0
        values = [
            jnp.where(low, a, b) + pltpu.roll(jnp.where(low, b, a), step, axis=0)
            for a, b in zip(values[0::2], values[1::2])
        ]
    return values[0]


def sample_slot(s, block_ref, total, sorted_ref, out_ref, table_ref):
    dense = PARTS * PY * DENSE
    width = PY * DENSE
    for c in range(PARTS):
        part = block_ref[c * PX * PY : c * PX * PY + width]
        high = part.astype(BF16)
        low = (part - high.astype(F32)).astype(BF16)
        at = c * width
        for k in range(2):
            table_ref[at : at + width, PZ * k : PZ * k + PZ] = high
            table_ref[dense + at : dense + at + width, PZ * k : PZ * k + PZ] = low
    per = WIDE // PZ
    row = lax.broadcasted_iota(jnp.int32, (PY, PZ), 0).astype(F32)
    depth = lax.broadcasted_iota(jnp.int32, (PZ, WIDE), 0).astype(F32).astype(BF16)

    def in_two(value):
        high = value.astype(BF16).astype(F32)
        return high, value - high

    def packed(value):
        return jnp.broadcast_to(value, (16, WIDE)).astype(BF16)[0:1]

    def step(i, carry):
        loads = [sorted_ref[s, i * per + j] for j in range(per)]
        wide = jnp.concatenate(loads, axis=1)
        along_z, iz = wide[2:3], wide[5:6]
        lower_high, lower_low = in_two(1.0 - along_z)
        upper_high, upper_low = in_two(along_z)
        none = jnp.zeros((), BF16)
        at_lower = depth == packed(iz)
        at_upper = depth == packed(iz + 1.0)
        high = jnp.where(at_lower, packed(lower_high), jnp.where(at_upper, packed(upper_high), none))
        low = jnp.where(at_lower, packed(lower_low), jnp.where(at_upper, packed(upper_low), none))
        product = jnp.dot(table_ref[...], jnp.concatenate([high, low], axis=0), preferred_element_type=F32)
        for j in range(per):
            fx, fy, fz, ix, iy, iz = [jnp.broadcast_to(loads[j][k : k + 1], (PY, PZ)) for k in range(6)]
            lower = jnp.clip(iz.astype(jnp.int32), 0, PZ - 2)
            upper = lower + 1
            weight_y = jnp.where(row == iy, 1.0 - fy, jnp.where(row == iy + 1.0, fy, 0.0))
            lanes = slice(PZ * j, PZ * j + PZ)
            totals = [None] * PARTS
            for x in range(PX):
                weight = weight_y * jnp.where(ix == float(x), 1.0 - fx, jnp.where(ix == float(x - 1), fx, 0.0))
                weight_lower, weight_upper = weight * (1.0 - fz), weight * fz
                for c in range(PARTS):
                    if x < DENSE:
                        at = c * width + x * PY
                        term = (product[at : at + PY, lanes] + product[dense + at : dense + at + PY, lanes]) * weight
                    else:
                        at = (c * PX + x) * PY
                        cells = block_ref[at : at + PY]
                        term = (
                            jnp.take_along_axis(cells, lower, axis=1, mode="promise_in_bounds") * weight_lower
                            + jnp.take_along_axis(cells, upper, axis=1, mode="promise_in_bounds") * weight_upper
                        )
                    totals[c] = term if x == 0 else totals[c] + term
            out_ref[s, i * per + j] = fold_rows(totals)
        return carry

    lax.fori_loop(0, (total + WIDE - 1) // WIDE, step, 0)


def sample_kernel(slots, lines, places, part, lead, blocks, again, row_ref, slab_ref, info_ref, sorted_ref, *refs):
    block_refs = refs[:blocks]
    out_ref, table_ref = refs[blocks + again :]
    last = info_ref.shape[1] - 1
    row = row_ref[0]
    found = jnp.int32(0)
    for b, (distance, over) in enumerate(places):
        owner = lax.rem(row // 2 + (lines - distance), lines) * 2 + lax.rem(row + over, 2)
        s = jnp.int32(-1)
        for k in range(slots):
            s = jnp.where(slab_ref[k] == owner, k, s)
        take = s >= 0
        if b < lead:
            is_lead = jnp.logical_and(take, found == 0)
            found = jnp.where(take, 1, found)
            take = is_lead if part is None else jnp.logical_and(take, jnp.logical_not(is_lead))
        at = b if part is None else b - part[0]
        if not 0 <= at < blocks:
            continue

        @pl.when(take)
        def _(s=s, at=at):
            total = info_ref[s, last] + info_ref[slots + s, last]
            sample_slot(s, block_refs[at], total, sorted_ref, out_ref, table_ref)


def sample(setting, part, blocks, row, slabs, info, ordered, before):
    again = 0 if before is None else 1
    return kernel_call(
        functools.partial(sample_kernel, *setting[:3], part, setting[3], len(blocks), again),
        jax.ShapeDtypeStruct(ordered.shape, F32),
        [SMEM] * 3 + [VMEM] * (1 + len(blocks) + again),
        [pltpu.VMEM((2 * PARTS * PY * DENSE, 2 * PZ), BF16)],
        {4 + len(blocks): 0} if again else None,
        cost=2.5 if part is None else 5.0,
    )(row, slabs, info, ordered, *blocks, *([before] if again else []))


def transpose_inverse(matrix):
    cof_00 = matrix[1][1] * matrix[2][2] - matrix[1][2] * matrix[2][1]
    cof_01 = -(matrix[1][0] * matrix[2][2] - matrix[1][2] * matrix[2][0])
    cof_02 = matrix[1][0] * matrix[2][1] - matrix[1][1] * matrix[2][0]
    cof_10 = -(matrix[0][1] * matrix[2][2] - matrix[0][2] * matrix[2][1])
    cof_11 = matrix[0][0] * matrix[2][2] - matrix[0][2] * matrix[2][0]
    cof_12 = -(matrix[0][0] * matrix[2][1] - matrix[0][1] * matrix[2][0])
    cof_20 = matrix[0][1] * matrix[1][2] - matrix[0][2] * matrix[1][1]
    cof_21 = -(matrix[0][0] * matrix[1][2] - matrix[0][2] * matrix[1][0])
    cof_22 = matrix[0][0] * matrix[1][1] - matrix[0][1] * matrix[1][0]
    determinant = matrix[0][0] * cof_00 + matrix[0][1] * cof_01 + matrix[0][2] * cof_02
    reciprocal = 1.0 / determinant
    return [
        [cof_00 * reciprocal, cof_01 * reciprocal, cof_02 * reciprocal],
        [cof_10 * reciprocal, cof_11 * reciprocal, cof_12 * reciprocal],
        [cof_20 * reciprocal, cof_21 * reciprocal, cof_22 * reciprocal],
    ]


def polar_factor(jacobian):
    rotation = jacobian
    for repeat in range(STEPS):
        inverse = transpose_inverse(rotation)
        rotation = [
            [0.5 * (rotation[first][second] + inverse[first][second]) for second in range(3)] for first in range(3)
        ]
    return rotation


def reorient(rotation, components):
    tensor = [
        [components[0], components[3], components[4]],
        [components[3], components[1], components[5]],
        [components[4], components[5], components[2]],
    ]
    left = [
        [
            rotation[first][0] * tensor[0][second]
            + rotation[first][1] * tensor[1][second]
            + rotation[first][2] * tensor[2][second]
            for second in range(3)
        ]
        for first in range(3)
    ]

    def entry(first, second):
        return (
            left[first][0] * rotation[second][0]
            + left[first][1] * rotation[second][1]
            + left[first][2] * rotation[second][2]
        )

    return [entry(0, 0), entry(1, 1), entry(2, 2), entry(0, 1), entry(0, 2), entry(1, 2)]


def pack_kernel(place_ref, table_hbm, field_hbm, swap_ref, cross_ref, near_ref, far_ref, field_ref, sems):
    odd = (place_ref[0] & 1) == 1
    odd_column = (place_ref[1] & 1) == 1
    cells = table_hbm.shape[0]
    half = field_ref.shape[1] // 2
    load_field = pltpu.make_async_copy(field_hbm, field_ref, sems.at[0])
    load_table = pltpu.make_async_copy(table_hbm, swap_ref.at[0:cells], sems.at[1])
    load_field.start()
    load_table.start()
    load_field.wait()
    for c in range(3):
        even_rows = field_ref[c, pl.ds(0, half, stride=2), :]
        odd_rows = field_ref[c, pl.ds(1, half, stride=2), :]
        swap_ref[cells + half * c : cells + half * c + half, :] = jnp.where(odd, even_rows, odd_rows)
        cross_ref[half * c : half * c + half, :] = jnp.where(odd, odd_rows, even_rows)
        turned = field_ref[c].T
        first, last = turned[0:1], turned[PZ - 1 : PZ]
        near_ref[c : c + 1, :] = jnp.where(odd_column, first, last)
        far_ref[c : c + 1, :] = jnp.where(odd_column, last, first)
    load_table.wait()


def rotation_kernel(place_ref, field_ref, swapped_ref, crossed_ref, near_ref, far_ref, out_ref, wide_ref, slope_ref, edge_ref):
    odd = (place_ref[0] & 1) == 1
    odd_column = (place_ref[1] & 1) == 1
    rows = field_ref.shape[1]
    half = rows // 2
    cells = swapped_ref.shape[0] - 3 * half
    edge_ref[...] = jnp.zeros_like(edge_ref)
    edge_ref[0:3, :] = jnp.where(odd_column, near_ref[...], far_ref[...])
    edge_ref[3:6, :] = jnp.where(odd_column, far_ref[...], near_ref[...])
    edges = edge_ref[...].T
    for c in range(3):
        wide_ref[c, 0:8, :] = jnp.zeros((8, PZ), F32)
        wide_ref[c, 8 : 8 + rows, :] = field_ref[c]
        wide_ref[c, 8 + rows : 16 + rows, :] = jnp.zeros((8, PZ), F32)
        even_rows = wide_ref[c, pl.ds(8, half, stride=2), :]
        odd_rows = wide_ref[c, pl.ds(9, half, stride=2), :]
        paired = swapped_ref[cells + half * c : cells + half * c + half, :]
        other = crossed_ref[half * c : half * c + half, :]
        slope_ref[c, pl.ds(0, half, stride=2), :] = 0.5 * (odd_rows - jnp.where(odd, paired, other))
        slope_ref[c, pl.ds(1, half, stride=2), :] = 0.5 * (jnp.where(odd, other, paired) - even_rows)
    lane = lax.broadcasted_iota(jnp.int32, (16, PZ), 1)
    for b in range(rows // 16):
        jacobian = []
        for c in range(3):
            at = 16 * b
            middle = field_ref[c, at : at + 16, :]
            after = pltpu.roll(middle, PZ - 1, axis=1)
            after = jnp.where(lane == PZ - 1, edges[at : at + 16, 3 + c : 4 + c], after)
            prior = pltpu.roll(middle, 1, axis=1)
            prior = jnp.where(lane == 0, edges[at : at + 16, c : c + 1], prior)
            slopes = [
                slope_ref[c, at : at + 16, :],
                0.5 * (after - prior),
                0.5 * (wide_ref[c, at + 10 : at + 26, :] - wide_ref[c, at + 6 : at + 22, :]),
            ]
            jacobian.append([slopes[d] + 1.0 if d == c else slopes[d] for d in range(3)])
        rotation = polar_factor(jacobian)
        for first in range(3):
            for second in range(3):
                out_ref[3 * first + second, at : at + 16, :] = rotation[first][second]


def along(values, axis, pairs):
    return lax.ppermute(values, axis, pairs)


def both_ways(pairs):
    return list(pairs) + [(b, a) for a, b in pairs]


def finish_kernel(slots, info_ref, slot_ref, pos_ref, samples_ref, rotation_ref, out_hbm, row_ref, out_ref, sems):
    groups = slot_ref.shape[0]
    lane = lax.broadcasted_iota(jnp.int32, (8, PZ), 1)
    stores = []
    for part in range(groups // SHARE):
        for g in range(part * SHARE, part * SHARE + SHARE):
            slot = jnp.broadcast_to(slot_ref[g : g + 1, :], (8, PZ))
            index = jnp.broadcast_to(pos_ref[g : g + 1, :], (8, PZ)) & (PZ - 1)
            result = None
            for s in range(slots):
                base = info_ref[s, g]
                offset, at = base & (PZ - 1), base >> 7
                both = jnp.where(lane >= offset, samples_ref[s, at], samples_ref[s, at + 1])
                value = jnp.take_along_axis(both, index, axis=1, mode="promise_in_bounds")
                result = value if s == 0 else jnp.where(slot == s, value, result)
            row_ref[8 * g : 8 * g + 8, :] = result
        for at in range(part * SHARE, part * SHARE + SHARE, 8):
            components = [row_ref[pl.ds(at * 8 + c, 8, stride=8), :] for c in range(PARTS)]
            rotation = [[rotation_ref[3 * m + n, at : at + 8, :] for n in range(3)] for m in range(3)]
            for c, value in enumerate(reorient(rotation, components)):
                out_ref[c, at : at + 8, :] = value
        here = pl.ds(part * SHARE, SHARE)
        stores.append(pltpu.make_async_copy(out_ref.at[:, here], out_hbm.at[:, here], sems.at[part]))
        stores[-1].start()
    for store in stores:
        store.wait()


def on_device(source, lists, voxel_slot, voxel_cell, frac, displace):
    count = lax.axis_size("bx")
    columns = lax.axis_size("by")
    row = lax.axis_index("bx")
    lines = count // 2
    slots = lists.shape[2]
    voxels = voxel_cell.shape[2]
    groups = voxels // PZ
    half = groups // 2
    cells = PARTS * PX * PY
    table = source.reshape(cells, PZ)
    field = displace.reshape(3, groups, PZ)
    here = jnp.stack([row, lax.axis_index("by")]).astype(jnp.int32)

    swap = [(i, i ^ 1) for i in range(count)]
    forward = [(i, (i + 2) % count) for i in range(count)]
    backward = [(b, a) for a, b in forward]
    line = jax.ShapeDtypeStruct((3, groups), F32)
    packed, facing, near_lane, far_lane = kernel_call(
        pack_kernel,
        (
            jax.ShapeDtypeStruct((cells + 3 * half, PZ), F32),
            jax.ShapeDtypeStruct((3 * half, PZ), F32),
            line,
            line,
        ),
        [SMEM, HBM, HBM],
        [pltpu.VMEM((3, groups, PZ), F32), pltpu.SemaphoreType.DMA((2,))],
    )(here, *[pltpu.with_memory_space_constraint(a, pltpu.HBM) for a in (table, field)])
    slot_rows = voxel_slot.reshape(groups, PZ)
    sent = table
    swapped = along(packed, "bx", swap)
    near = along(near_lane, "by", both_ways([(i, i + 1) for i in range(0, columns - 1, 2)]))
    far = along(far_lane, "by", both_ways([(i, i + 1) for i in range(1, columns - 1, 2)]))
    ahead = along(sent, "bx", forward)
    behind = along(sent, "bx", backward)

    ints = functools.partial(jax.ShapeDtypeStruct, dtype=jnp.int32)
    ordered, pos, info = kernel_call(
        functools.partial(order_kernel, slots),
        (
            jax.ShapeDtypeStruct((slots, groups + WIDE // PZ + 1, 8, PZ), F32),
            ints((groups, PZ)),
            ints((2 * slots, groups)),
        ),
        [HBM] * 3,
        [
            pltpu.VMEM((groups, PZ), jnp.int32),
            pltpu.VMEM((groups, PZ), jnp.int32),
            pltpu.VMEM((3, groups, PZ), F32),
            pltpu.VMEM((groups, PZ), jnp.int32),
            pltpu.VMEM((groups * 8, PZ), F32),
            pltpu.VMEM((groups, 8, PZ), jnp.int32),
            pltpu.SMEM((2 * slots, groups), jnp.int32),
            pltpu.SemaphoreType.DMA((4,)),
        ],
        cost=7.0,
    )(*[
        pltpu.with_memory_space_constraint(a, pltpu.HBM)
        for a in (slot_rows, voxel_cell.reshape(groups, PZ), frac.reshape(3, groups, PZ))
    ])
    facing, swapped, ordered = lax.optimization_barrier((facing, swapped, ordered))
    crossed = along(facing, "bx", both_ways([(i, i + 1) for i in range(1, count - 1, 2)]))
    ahead, behind, near_lane, far_lane, ordered = lax.optimization_barrier((ahead, behind, near, far, ordered))

    near = {1: ahead}
    if lines > 2:
        near[-1] = behind
    far = {}
    for k in range(2, lines // 2 + 1):
        far[k] = ahead = along(ahead, "bx", forward)
        if 2 * k < lines:
            far[-k] = behind = along(behind, "bx", backward)
    near_over = {k: along(block, "bx", swap) for k, block in near.items()}

    my_slabs = lax.dynamic_index_in_dim(lists[:, 0, :], row, 0, keepdims=False)
    places = [(0, 0), (0, 1)] + [(k, 0) for k in (*near, *far)] + [(k, 1) for k in (*near, *far)]
    blocks = [packed, swapped, *near.values()]
    setting = (slots, lines, places, len(blocks))
    samples = sample(setting, None, blocks, here, my_slabs, info, ordered, None)
    if far:
        *later, samples = lax.optimization_barrier((*far.values(), samples))
        far = dict(zip(far, later))
    far_over = {k: along(block, "bx", swap) for k, block in far.items()}
    blocks += far.values()
    samples = sample(setting, (0, len(blocks)), blocks, here, my_slabs, info, ordered, samples)
    for over in (near_over, far_over):
        first = len(blocks)
        blocks += over.values()
        if over:
            samples = sample(setting, (first, len(blocks)), [*over.values()], here, my_slabs, info, ordered, samples)
        if over is near_over:
            crossed, samples = lax.optimization_barrier((crossed, samples))

    rotation = kernel_call(
        rotation_kernel,
        jax.ShapeDtypeStruct((9, groups, PZ), F32),
        [SMEM] + [VMEM] * 5,
        [
            pltpu.VMEM((3, groups + 16, PZ), F32),
            pltpu.VMEM((3, groups, PZ), F32),
            pltpu.VMEM((8, groups), F32),
        ],
    )(here, field, swapped, crossed, near_lane, far_lane)

    result = kernel_call(
        functools.partial(finish_kernel, slots),
        jax.ShapeDtypeStruct((PARTS, groups, PZ), F32),
        [SMEM] + [VMEM] * 4,
        [
            pltpu.VMEM((groups * 8, PZ), F32),
            pltpu.VMEM((PARTS, groups, PZ), F32),
            pltpu.SemaphoreType.DMA((groups // SHARE,)),
        ],
        out_spec=HBM,
    )(info, slot_rows, pos, samples, rotation)
    return result.reshape(1, 1, PARTS, voxels)


def solution(mesh):
    return jax.shard_map(
        on_device,
        mesh=mesh,
        in_specs=(
            P("bx", "by", None, None),
            P(None, "by", None),
            P("bx", "by", None),
            P("bx", "by", None),
            P("bx", "by", None, None),
            P(None, None, "bx", "by"),
        ),
        out_specs=P("bx", "by", None, None),
        check_vma=False,
    )
```
